32 devices in a mesh: blk: 4 (over z), grp: 8 (over y, x, core).
Axes of the slice: x: 2, y: 2, z: 4, core: 2. Of those that a mesh axis runs over, the one named last changes fastest.
Arguments:
- obj_query: bfloat16 [2048, 1536], P(('blk', 'grp')), may hold values from -64 to 64
- grad_out: bfloat16 [2048, 1536], P(('blk', 'grp')), may hold values from -256 to 256
- pattern_key: bfloat16 [2048, 1536], P('grp'), may hold values from -4.5 to 4.5
- pattern_value: bfloat16 [2048, 1536], P('grp'), may hold values from -6 to 6
- pencil_order: int32 [128], replicated, may hold values from 0 to 127, as said below
Outputs:
- query_grad: bfloat16 [2048, 1536], P(('blk', 'grp'))
- key_grad: bfloat16 [2048, 1536], P(('blk', 'grp'))
- value_grad: bfloat16 [2048, 1536], P(('blk', 'grp'))
The draws below stay inside these ranges and needn't reach their ends.
Inputs may be any that keep to these rules, and one draw needn't show every extreme that they name: pencil_order is a permutation of 0 to 127. With c the number of devices along grp, block r of the encoder's layout lies on the device of index r // 4 of the axes blk+grp, and pencil_order[r] names a block of pattern rows g * 256 to (g + 1) * 256 - 1, where g is that device index mod c.
All inputs are finite; a program needn't handle non-finite values.
Results may differ from the reference program's by a relative error of at most 0.0051.
Values may be sent and summed in bfloat16 or wider, within the bound.
A program may use at most 128 MiB of HBM per device.

```python
import math
import jax
import jax.numpy as jnp
from jax import lax

D = 1536
H = 16
PD = 64
PENCIL = 16
NQ = 2048
NK = 2048
N_BLK = 4
N_GRP = 8


def base_keys(key):
    inner_key = jax.random.fold_in(key, 7)
    key_table = jnp.clip(jax.random.normal(inner_key, (NK, D), jnp.float32), -4.5, 4.5)
    return key_table.astype(jnp.bfloat16).astype(jnp.float32)


def draw_pattern_key(key, part):
    return base_keys(key).astype(jnp.bfloat16)


def draw_obj_query(key, part):
    inner_key = jax.random.fold_in(key, 11)
    query_table = jnp.clip(jax.random.normal(inner_key, (NQ, D), jnp.float32), -4.5, 4.5)
    return query_table.astype(jnp.bfloat16)


def draw_pencil_order(key, part):
    per_block = PD // PENCIL
    column_blocks = N_BLK * per_block

    def column_order(column):
        return jax.random.permutation(jax.random.fold_in(key, column), column_blocks)
    orders = jax.vmap(column_order)(jnp.arange(N_GRP, dtype=jnp.int32))
    blocks = jnp.arange(NK // PENCIL, dtype=jnp.int32)
    device = blocks // per_block
    column = device % N_GRP
    chosen = orders[column, device // N_GRP * per_block + blocks % per_block]
    return (column * column_blocks + chosen).astype(jnp.int32)


def level_of(own_key, dims, cuts, smallest, top_value):
    loudness, own = 1.0, jax.random.fold_in(own_key, 6)
    for position, blocks in cuts:
        steps = jnp.exp(jax.random.uniform(jax.random.fold_in(own, position), (blocks,), jnp.float32, smallest / len(cuts), top_value / len(cuts)))
        loudness = loudness * jnp.repeat(steps, dims[position] // blocks).reshape([-1 if axis == position else 1 for axis in range(len(dims))])
    return loudness


def gaussian(key, dims, deviation, limit, cuts=(), kind=jnp.bfloat16):
    entries = deviation * jax.random.normal(key, dims, jnp.float32)
    if cuts:
        entries = entries * level_of(key, dims, cuts, -0.22, 0.18)
    return jnp.clip(entries, -limit, limit).astype(kind)


def setup_inputs(seed: int = 0) -> dict:
    key_list = jax.random.split(jax.random.key(seed), 6)
    obj_query = draw_obj_query(jax.random.fold_in(key_list[5], 71), 0)
    grad_out = gaussian(key_list[1], (NQ, D), 48, 256.0, ((0, 32),))
    pattern_key = draw_pattern_key(jax.random.fold_in(key_list[5], 71), 0)
    pattern_value = gaussian(key_list[3], (NK, D), 1.0, 6.0, ((0, 8),))
    pencil_order = draw_pencil_order(jax.random.fold_in(key_list[5], 71), 0)
    return {"obj_query": obj_query, "grad_out": grad_out, "pattern_key": pattern_key, "pattern_value": pattern_value, "pencil_order": pencil_order}


def split_heads(matrix):
    return matrix.reshape(matrix.shape[0], H, matrix.shape[1] // H)

def reference(obj_query, grad_out, pattern_key, pattern_value, pencil_order):
    scaling = 1.0 / math.sqrt(D // H)
    key_heads = split_heads(pattern_key.astype(jnp.float32))
    value_heads = split_heads(pattern_value.astype(jnp.float32))
    blocking = math.gcd(NQ, 256)
    sweeps = NQ // blocking

    def sweep(carried, segment):
        keys_acc, values_acc = carried
        query_heads = split_heads(segment[0].astype(jnp.float32))
        grad_heads = split_heads(segment[1].astype(jnp.float32))
        scores = jnp.einsum('rhd,chd->hrc', query_heads, key_heads) * scaling
        prob_grad = jnp.einsum('rhd,chd->hrc', grad_heads, value_heads)
        highest = lax.optimization_barrier(jnp.max(scores, axis=2))
        weights = jnp.exp(scores - highest[:, :, None])
        totals = lax.optimization_barrier(jnp.sum(weights, axis=2))
        log_totals = highest + jnp.log(totals)
        mean_grads = lax.optimization_barrier(jnp.sum(weights * prob_grad, axis=2)) / totals
        softmax = jnp.exp(scores - log_totals[:, :, None])
        softmax_low = lax.optimization_barrier(softmax.astype(jnp.bfloat16)).astype(jnp.float32)
        score_grad = lax.optimization_barrier((scaling * softmax * (prob_grad - mean_grads[:, :, None])).astype(jnp.bfloat16)).astype(jnp.float32)
        query_term = jnp.einsum('hrc,chd->rhd', score_grad, key_heads).reshape(blocking, D)
        keys_acc = keys_acc + jnp.einsum('hrc,rhd->chd', score_grad, query_heads).reshape(NK, D)
        values_acc = values_acc + jnp.einsum('hrc,rhd->chd', softmax_low, grad_heads).reshape(NK, D)
        return ((keys_acc, values_acc), query_term.astype(jnp.bfloat16))
    zeros_acc = jnp.zeros((NK, D), jnp.float32)
    segments = (obj_query.reshape(sweeps, blocking, D), grad_out.reshape(sweeps, blocking, D))
    (keys_acc, values_acc), pieces = lax.scan(sweep, (zeros_acc, zeros_acc), segments)
    positions = jnp.arange(NK, dtype=jnp.int32)
    source = (pencil_order[positions // PENCIL] * PENCIL + positions % PENCIL).astype(jnp.int32)
    query_grad = pieces.reshape(NQ, D)
    key_grad = keys_acc[source].astype(jnp.bfloat16)
    value_grad = values_acc[source].astype(jnp.bfloat16)
    return (query_grad, key_grad, value_grad)
```

```python
import functools
import math

import jax
import jax.numpy as jnp
from jax import lax
from jax.experimental import pallas as pl
from jax.experimental.pallas import tpu as pltpu
from jax.sharding import PartitionSpec as P

H = 16
PENCIL = 16


def joined(value, axis, combine):
    everything = jax.tree.map(lambda part: lax.all_gather(part, axis), value)
    initial = jax.tree.map(lambda part: part[0], everything)

    def step(k, so_far):
        return combine(so_far, jax.tree.map(lambda part: part[k], everything))

    return lax.fori_loop(1, lax.axis_size(axis), step, initial)


def split_heads(matrix):
    return matrix.reshape(matrix.shape[0], H, matrix.shape[1] // H)


def block_stats(part_query, part_grad, key_block, value_block):
    scaling = 1.0 / math.sqrt(key_block.shape[1] // H)
    scores = (
        jnp.einsum(
            "rhd,chd->hrc",
            split_heads(part_query),
            split_heads(key_block),
            preferred_element_type=jnp.float32,
        )
        * scaling
    )
    prob_grad = jnp.einsum(
        "rhd,chd->hrc",
        split_heads(part_grad),
        split_heads(value_block),
        preferred_element_type=jnp.float32,
    )
    highest = jnp.max(scores, axis=2)
    weights = jnp.exp(scores - highest[:, :, None])
    return (highest, jnp.sum(weights, axis=2), jnp.sum(weights * prob_grad, axis=2))


def join_stats(earlier, later):
    highest = jnp.maximum(earlier[0], later[0])
    before = jnp.exp(earlier[0] - highest)
    after = jnp.exp(later[0] - highest)
    return (highest, earlier[1] * before + later[1] * after, earlier[2] * before + later[2] * after)


def stats_of_rows(queries, grads, key_block, value_block):
    amount, features = queries.shape
    blocking = math.gcd(amount, 128)

    def one_block(couple):
        return block_stats(couple[0], couple[1], key_block, value_block)

    stacked = lax.map(
        one_block,
        (
            queries.reshape(amount // blocking, blocking, features),
            grads.reshape(amount // blocking, blocking, features),
        ),
    )
    return tuple((jnp.moveaxis(member, 0, 1).reshape(H, amount) for member in stacked))


def block_grads(part_query, part_grad, log_now, mean_now, key_block, value_block):
    features = key_block.shape[1]
    scaling = 1.0 / math.sqrt(features // H)
    query_heads = split_heads(part_query)
    grad_heads = split_heads(part_grad)
    key_heads = split_heads(key_block)
    value_heads = split_heads(value_block)
    scores = (
        jnp.einsum("rhd,chd->hrc", query_heads, key_heads, preferred_element_type=jnp.float32)
        * scaling
    )
    prob_grad = jnp.einsum(
        "rhd,chd->hrc", grad_heads, value_heads, preferred_element_type=jnp.float32
    )
    softmax = jnp.exp(scores - log_now[:, :, None])
    softmax_low = softmax.astype(jnp.bfloat16)
    score_grad = (scaling * softmax * (prob_grad - mean_now[:, :, None])).astype(jnp.bfloat16)
    query_term = jnp.einsum(
        "hrc,chd->rhd", score_grad, key_heads, preferred_element_type=jnp.float32
    ).reshape(part_query.shape[0], features)
    key_term = jnp.einsum(
        "hrc,rhd->chd", score_grad, query_heads, preferred_element_type=jnp.float32
    ).reshape(key_block.shape[0], features)
    value_term = jnp.einsum(
        "hrc,rhd->chd", softmax_low, grad_heads, preferred_element_type=jnp.float32
    ).reshape(key_block.shape[0], features)
    return (query_term, key_term, value_term)


def on_device(obj_query, grad_out, pattern_key, pattern_value, pencil_order):
    amount, features = obj_query.shape
    columns = pattern_key.shape[0]
    groups = lax.axis_size("grp")
    position = lax.axis_index("grp")
    group_rows = groups * amount
    all_query, all_grad = (
        lax.all_gather(obj_query, "grp", axis=0, tiled=True),
        lax.all_gather(grad_out, "grp", axis=0, tiled=True),
    )
    partial_value = stats_of_rows(all_query, all_grad, pattern_key, pattern_value)
    highest, totals, weighted = joined(partial_value, "grp", join_stats)
    log_totals = highest + jnp.log(totals)
    mean_grads = weighted / totals
    blocking = math.gcd(group_rows, 128)
    sweeps = group_rows // blocking

    def sweep(carried, segment):
        keys_acc, values_acc = carried
        query_term, key_term, value_term = block_grads(
            segment[0], segment[1], segment[2], segment[3], pattern_key, pattern_value
        )
        return ((keys_acc + key_term, values_acc + value_term), query_term)

    log_blocks = jnp.moveaxis(log_totals.reshape(H, sweeps, blocking), 1, 0)
    mean_blocks = jnp.moveaxis(mean_grads.reshape(H, sweeps, blocking), 1, 0)
    zeros_acc = jnp.zeros((columns, features), jnp.float32)
    segments = (
        all_query.reshape(sweeps, blocking, features),
        all_grad.reshape(sweeps, blocking, features),
        log_blocks,
        mean_blocks,
    )
    (keys_acc, values_acc), pieces = lax.scan(sweep, (zeros_acc, zeros_acc), segments)
    query_total = lax.psum_scatter(
        pieces.reshape(group_rows, features), "grp", scatter_dimension=0, tiled=True
    )
    device_rows = columns // lax.axis_size("blk")
    spots = jnp.arange(columns, dtype=jnp.int32)
    target = (spots // device_rows * groups + position) * device_rows + spots % device_rows
    source = (
        jnp.take(pencil_order, target // PENCIL) * PENCIL + target % PENCIL - position * columns
    )
    combined = lax.psum_scatter(
        jnp.concatenate(
            [jnp.take(keys_acc, source, axis=0), jnp.take(values_acc, source, axis=0)], axis=1
        ),
        "blk",
        scatter_dimension=0,
        tiled=True,
    )
    key_grad = combined[:, :features].astype(jnp.bfloat16)
    value_grad = combined[:, features:].astype(jnp.bfloat16)
    return (query_total.astype(jnp.bfloat16), key_grad, value_grad)


MESH = pl.DeviceIdType.MESH
F32 = jnp.float32
BF16 = jnp.bfloat16


def mm(a, b, ca, cb):
    return lax.dot_general(a, b, (((ca,), (cb,)), ((), ())), preferred_element_type=F32)


def turn(x):
    return x.T


def fused(
    n_blk,
    n_grp,
    hd,
    q_ref,
    g_ref,
    k_ref,
    v_ref,
    order_ref,
    oq_ref,
    ok_ref,
    ov_ref,
    kvt_own,
    kvt,
    qz,
    qgt_own,
    qgt,
    s_buf,
    d_buf,
    kvacc,
    kvsend,
    rkv,
    pst,
    full_kv,
    qg,
    qst,
    full_q,
    onehot,
    zst,
    kv_ss,
    kv_rs,
    z_ss,
    z_rs,
    pq_ss,
    pq_rs,
    r_ss,
    r_rs,
    pk_ss,
    pk_rs,
    po_ss,
    po_rs,
    o_ss,
    o_rs,
):
    b = lax.axis_index("blk")
    g = lax.axis_index("grp")
    chips = n_grp // 2
    p = g // 2
    c = g % 2
    partner = 2 * p + 1 - c
    rows = q_ref.shape[0]
    cols = k_ref.shape[0]
    nk = cols * n_grp
    gw = 4 * hd
    scaling = 1.0 / math.sqrt(hd)
    expc = scaling * math.log2(math.e)

    def lanes(index, width):
        return pl.ds(pl.multiple_of(index * width, width), width)

    def remote(src, dst, ss, rs, bb, gg):
        copy = pltpu.make_async_remote_copy(
            src_ref=src,
            dst_ref=dst,
            send_sem=ss,
            recv_sem=rs,
            device_id=(bb, gg),
            device_id_type=MESH,
        )
        copy.start()
        return copy

    barrier = pltpu.get_barrier_semaphore()
    for d in range(1, n_grp):
        pl.semaphore_signal(barrier, inc=1, device_id=(b, (g + d) % n_grp), device_id_type=MESH)
    for d in range(1, n_blk):
        pl.semaphore_signal(barrier, inc=1, device_id=((b + d) % n_blk, g), device_id_type=MESH)

    for t, ref in enumerate((k_ref, v_ref)):
        part = turn(ref[:, lanes(b, gw)])
        for hl in range(4):
            kvt_own[hl, t] = part[hd * hl : hd * hl + hd]
    pl.semaphore_wait(barrier, n_grp + n_blk - 2)

    z_copies = []
    for d in range(1, n_blk):
        bb = (b + d) % n_blk
        for t, ref in enumerate((q_ref, g_ref)):
            z_copies.append(
                remote(
                    ref.at[:, lanes(bb, gw)],
                    qz.at[t, lanes(b, rows), :],
                    z_ss.at[d - 1, t],
                    z_rs.at[d - 1, t],
                    bb,
                    g,
                )
            )
    kv_copies = {}
    for h in range(2):
        for d in range(1, n_grp):
            gg = (g + d) % n_grp
            kv_copies[h, d] = remote(
                kvt_own.at[2 * (gg % 2) + h],
                kvt.at[h, :, :, lanes(g, cols)],
                kv_ss.at[d - 1, h],
                kv_rs.at[d - 1, h],
                b,
                gg,
            )
    for h in range(2):
        for t in range(2):
            kvt[h, t, :, lanes(g, cols)] = kvt_own[2 * c + h, t]
    for t, ref in enumerate((q_ref, g_ref)):
        qz[t, lanes(b, rows), :] = ref[:, lanes(b, gw)]

    row = lax.broadcasted_iota(jnp.int32, (PENCIL, cols), 0)
    col = lax.broadcasted_iota(jnp.int32, (PENCIL, cols), 1)
    per = rows // PENCIL
    for bb in range(n_blk):
        for k in range(per):
            first = order_ref[(bb * n_grp + g) * per + k] * PENCIL - g * cols
            onehot[pl.ds(bb * rows + k * PENCIL, PENCIL), :] = jnp.where(
                col - row == first, 1.0, 0.0
            ).astype(BF16)

    for copy in z_copies:
        copy.wait_recv()
    for t in range(2):
        part = turn(qz[t])
        for hl in range(4):
            qgt_own[hl, t] = part[hd * hl : hd * hl + hd]
    pair_q = remote(
        qgt_own.at[pl.ds(2 * (1 - c), 2)],
        qgt.at[:, :, :, lanes(c, cols)],
        pq_ss,
        pq_rs,
        b,
        partner,
    )
    for h in range(2):
        for t in range(2):
            qgt[h, t, :, lanes(c, cols)] = qgt_own[2 * c + h, t]
    pair_q.wait_recv()

    r_copies = {}
    wide = 256
    for h in range(2):
        for d in range(1, n_grp):
            kv_copies[h, d].wait_recv()
        kvacc[h] = jnp.zeros_like(kvacc[h])

        def block(j, carry):
            qt = qgt[h, 0, :, lanes(j, cols)]
            gt = qgt[h, 1, :, lanes(j, cols)]
            qb = turn(qt)
            gb = turn(gt)
            top = jnp.full((cols, wide), -jnp.inf, F32)
            for n in range(nk // wide):
                at = pl.ds(n * wide, wide)
                s = mm(qb, kvt[h, 0, :, at], 1, 0)
                s_buf[:, at] = s
                top = jnp.maximum(top, s)
            top = jnp.max(top, axis=1, keepdims=True)
            tot = jnp.zeros((cols, wide), F32)
            wtd = jnp.zeros((cols, wide), F32)
            for n in range(nk // wide):
                at = pl.ds(n * wide, wide)
                e = jnp.exp2((s_buf[:, at] - top) * expc)
                dp = mm(gb, kvt[h, 1, :, at], 1, 0)
                s_buf[:, at] = e
                d_buf[:, at] = dp
                tot = tot + e
                wtd = wtd + e * dp
            inv = 1.0 / jnp.sum(tot, axis=1, keepdims=True)
            mean = jnp.sum(wtd, axis=1, keepdims=True) * inv
            acc = jnp.zeros((cols, hd), F32)
            for n in range(nk // wide):
                at = pl.ds(n * wide, wide)
                soft = s_buf[:, at] * inv
                low = soft.astype(BF16)
                sg = (scaling * soft * (d_buf[:, at] - mean)).astype(BF16)
                kvacc[h, 0, :, at] += mm(qt, sg, 1, 0)
                kvacc[h, 1, :, at] += mm(gt, low, 1, 0)
                acc = acc + mm(sg, kvt[h, 0, :, at], 1, 1)
            qg[h, lanes(j, cols), :] = acc
            return carry

        lax.fori_loop(0, 2, block, 0)
        kvsend[h] = kvacc[h].astype(BF16)
        for e in range(1, chips):
            pp = (p + e) % chips
            r_copies[h, e] = remote(
                kvsend.at[h, :, :, lanes(pp, 2 * cols)],
                rkv.at[e - 1, h],
                r_ss.at[e - 1, h],
                r_rs.at[e - 1, h],
                b,
                2 * pp + c,
            )

    for h in range(2):
        qst[h] = turn(qg[h, lanes(1 - c, cols), :]).astype(BF16)
    pair_o = remote(qst, full_q.at[pl.ds(2 * c, 2)], po_ss, po_rs, b, partner)
    for h in range(2):
        full_q[2 * c + h] = turn(qg[h, lanes(c, cols), :]).astype(BF16)
    pair_o.wait_recv()

    out_copies = []

    def deliver(t, value, out):
        zst[t] = value
        for d in range(1, n_blk):
            bb = (b + d) % n_blk
            out_copies.append(
                remote(
                    zst.at[t, lanes(bb, rows), :],
                    out.at[:, lanes(b, gw)],
                    o_ss.at[d - 1, t],
                    o_rs.at[d - 1, t],
                    bb,
                    g,
                )
            )
        out[:, lanes(b, gw)] = zst[t, lanes(b, rows), :]

    deliver(0, turn(full_q[...].reshape(gw, cols)), oq_ref)

    pair_k = []
    for h in range(2):
        for e in range(1, chips):
            r_copies[h, e].wait_recv()

        def summed(part):
            at = pl.ds(pl.multiple_of(p * 2 * cols + part * cols, cols), cols)
            total = kvacc[h, :, :, at]
            for e in range(1, chips):
                total = total + rkv[e - 1, h, :, :, lanes(part, cols)].astype(F32)
            return total.astype(BF16)

        pst[h] = summed(1 - c)
        pair_k.append(
            remote(pst.at[h], full_kv.at[2 * c + h], pk_ss.at[h], pk_rs.at[h], b, partner)
        )
        full_kv[2 * c + h] = summed(c)
    for copy in pair_k:
        copy.wait_recv()
    for t, out in enumerate((ok_ref, ov_ref)):
        both = full_kv[:, t].reshape(gw, cols)
        deliver(1 + t, mm(onehot[...], both, 1, 1).astype(BF16), out)

    for copy in out_copies:
        copy.wait_recv()
    for copy in [*z_copies, *kv_copies.values(), *r_copies.values(), *pair_k, *out_copies]:
        copy.wait_send()
    pair_q.wait_send()
    pair_o.wait_send()


def fused_on_device(n_blk, n_grp, obj_query, grad_out, pattern_key, pattern_value, pencil_order):
    rows, features = obj_query.shape
    cols = pattern_key.shape[0]
    hd = features // H
    nk = cols * n_grp
    chips = n_grp // 2
    gw = 4 * hd
    dma = pltpu.SemaphoreType.DMA
    vmem = pl.BlockSpec(memory_space=pltpu.VMEM)
    return tuple(
        pl.pallas_call(
            functools.partial(fused, n_blk, n_grp, hd),
            out_shape=[jax.ShapeDtypeStruct((rows, features), BF16)] * 3,
            in_specs=[vmem] * 4 + [pl.BlockSpec(memory_space=pltpu.SMEM)],
            out_specs=[vmem] * 3,
            scratch_shapes=[
                pltpu.VMEM((4, 2, hd, cols), BF16),
                pltpu.VMEM((2, 2, hd, nk), BF16),
                pltpu.VMEM((2, cols, gw), BF16),
                pltpu.VMEM((4, 2, hd, cols), BF16),
                pltpu.VMEM((2, 2, hd, 2 * cols), BF16),
                pltpu.VMEM((cols, nk), F32),
                pltpu.VMEM((cols, nk), F32),
                pltpu.VMEM((2, 2, hd, nk), F32),
                pltpu.VMEM((2, 2, hd, nk), BF16),
                pltpu.VMEM((chips - 1, 2, 2, hd, 2 * cols), BF16),
                pltpu.VMEM((2, 2, hd, cols), BF16),
                pltpu.VMEM((4, 2, hd, cols), BF16),
                pltpu.VMEM((2, 2 * cols, hd), F32),
                pltpu.VMEM((2, hd, cols), BF16),
                pltpu.VMEM((4, hd, cols), BF16),
                pltpu.VMEM((cols, cols), BF16),
                pltpu.VMEM((3, cols, gw), BF16),
                dma((n_grp - 1, 2)),
                dma((n_grp - 1, 2)),
                dma((n_blk - 1, 2)),
                dma((n_blk - 1, 2)),
                dma,
                dma,
                dma((chips - 1, 2)),
                dma((chips - 1, 2)),
                dma((2,)),
                dma((2,)),
                dma,
                dma,
                dma((n_blk - 1, 3)),
                dma((n_blk - 1, 3)),
            ],
            compiler_params=pltpu.CompilerParams(
                collective_id=0, has_side_effects=True, vmem_limit_bytes=48 * 1024 * 1024
            ),
        )(obj_query, grad_out, pattern_key, pattern_value, pencil_order)
    )


def solution(mesh):
    in_specs = (
        P(("blk", "grp"), None),
        P(("blk", "grp"), None),
        P("grp", None),
        P("grp", None),
        P(),
    )
    out_specs = (P(("blk", "grp"), None), P(("blk", "grp"), None), P(("blk", "grp"), None))
    n_blk, n_grp = mesh.shape["blk"], mesh.shape["grp"]

    def body(obj_query, grad_out, pattern_key, pattern_value, pencil_order):
        features = obj_query.shape[1]
        fits = (
            n_blk * 4 == H
            and (features // n_blk) % 128 == 0
            and pattern_key.shape[0] == 256
            and n_blk * obj_query.shape[0] == 256
        )
        step = functools.partial(fused_on_device, n_blk, n_grp) if fits else on_device
        return step(obj_query, grad_out, pattern_key, pattern_value, pencil_order)

    return jax.shard_map(body, mesh=mesh, in_specs=in_specs, out_specs=out_specs, check_vma=False)
```

```python
import functools
import math

import jax
import jax.numpy as jnp
from jax import lax
from jax.experimental import pallas as pl
from jax.experimental.pallas import tpu as pltpu
from jax.sharding import PartitionSpec as P

H = 16
PENCIL = 16


def joined(value, axis, combine):
    everything = jax.tree.map(lambda part: lax.all_gather(part, axis), value)
    initial = jax.tree.map(lambda part: part[0], everything)

    def step(k, so_far):
        return combine(so_far, jax.tree.map(lambda part: part[k], everything))

    return lax.fori_loop(1, lax.axis_size(axis), step, initial)


def split_heads(matrix):
    return matrix.reshape(matrix.shape[0], H, matrix.shape[1] // H)


def block_stats(part_query, part_grad, key_block, value_block):
    scaling = 1.0 / math.sqrt(key_block.shape[1] // H)
    scores = (
        jnp.einsum(
            "rhd,chd->hrc",
            split_heads(part_query),
            split_heads(key_block),
            preferred_element_type=jnp.float32,
        )
        * scaling
    )
    prob_grad = jnp.einsum(
        "rhd,chd->hrc",
        split_heads(part_grad),
        split_heads(value_block),
        preferred_element_type=jnp.float32,
    )
    highest = jnp.max(scores, axis=2)
    weights = jnp.exp(scores - highest[:, :, None])
    return (highest, jnp.sum(weights, axis=2), jnp.sum(weights * prob_grad, axis=2))


def join_stats(earlier, later):
    highest = jnp.maximum(earlier[0], later[0])
    before = jnp.exp(earlier[0] - highest)
    after = jnp.exp(later[0] - highest)
    return (highest, earlier[1] * before + later[1] * after, earlier[2] * before + later[2] * after)


def stats_of_rows(queries, grads, key_block, value_block):
    amount, features = queries.shape
    blocking = math.gcd(amount, 128)

    def one_block(couple):
        return block_stats(couple[0], couple[1], key_block, value_block)

    stacked = lax.map(
        one_block,
        (
            queries.reshape(amount // blocking, blocking, features),
            grads.reshape(amount // blocking, blocking, features),
        ),
    )
    return tuple((jnp.moveaxis(member, 0, 1).reshape(H, amount) for member in stacked))


def block_grads(part_query, part_grad, log_now, mean_now, key_block, value_block):
    features = key_block.shape[1]
    scaling = 1.0 / math.sqrt(features // H)
    query_heads = split_heads(part_query)
    grad_heads = split_heads(part_grad)
    key_heads = split_heads(key_block)
    value_heads = split_heads(value_block)
    scores = (
        jnp.einsum("rhd,chd->hrc", query_heads, key_heads, preferred_element_type=jnp.float32)
        * scaling
    )
    prob_grad = jnp.einsum(
        "rhd,chd->hrc", grad_heads, value_heads, preferred_element_type=jnp.float32
    )
    softmax = jnp.exp(scores - log_now[:, :, None])
    softmax_low = softmax.astype(jnp.bfloat16)
    score_grad = (scaling * softmax * (prob_grad - mean_now[:, :, None])).astype(jnp.bfloat16)
    query_term = jnp.einsum(
        "hrc,chd->rhd", score_grad, key_heads, preferred_element_type=jnp.float32
    ).reshape(part_query.shape[0], features)
    key_term = jnp.einsum(
        "hrc,rhd->chd", score_grad, query_heads, preferred_element_type=jnp.float32
    ).reshape(key_block.shape[0], features)
    value_term = jnp.einsum(
        "hrc,rhd->chd", softmax_low, grad_heads, preferred_element_type=jnp.float32
    ).reshape(key_block.shape[0], features)
    return (query_term, key_term, value_term)


def on_device(obj_query, grad_out, pattern_key, pattern_value, pencil_order):
    amount, features = obj_query.shape
    columns = pattern_key.shape[0]
    groups = lax.axis_size("grp")
    position = lax.axis_index("grp")
    group_rows = groups * amount
    all_query, all_grad = (
        lax.all_gather(obj_query, "grp", axis=0, tiled=True),
        lax.all_gather(grad_out, "grp", axis=0, tiled=True),
    )
    partial_value = stats_of_rows(all_query, all_grad, pattern_key, pattern_value)
    highest, totals, weighted = joined(partial_value, "grp", join_stats)
    log_totals = highest + jnp.log(totals)
    mean_grads = weighted / totals
    blocking = math.gcd(group_rows, 128)
    sweeps = group_rows // blocking

    def sweep(carried, segment):
        keys_acc, values_acc = carried
        query_term, key_term, value_term = block_grads(
            segment[0], segment[1], segment[2], segment[3], pattern_key, pattern_value
        )
        return ((keys_acc + key_term, values_acc + value_term), query_term)

    log_blocks = jnp.moveaxis(log_totals.reshape(H, sweeps, blocking), 1, 0)
    mean_blocks = jnp.moveaxis(mean_grads.reshape(H, sweeps, blocking), 1, 0)
    zeros_acc = jnp.zeros((columns, features), jnp.float32)
    segments = (
        all_query.reshape(sweeps, blocking, features),
        all_grad.reshape(sweeps, blocking, features),
        log_blocks,
        mean_blocks,
    )
    (keys_acc, values_acc), pieces = lax.scan(sweep, (zeros_acc, zeros_acc), segments)
    query_total = lax.psum_scatter(
        pieces.reshape(group_rows, features), "grp", scatter_dimension=0, tiled=True
    )
    device_rows = columns // lax.axis_size("blk")
    spots = jnp.arange(columns, dtype=jnp.int32)
    target = (spots // device_rows * groups + position) * device_rows + spots % device_rows
    source = (
        jnp.take(pencil_order, target // PENCIL) * PENCIL + target % PENCIL - position * columns
    )
    combined = lax.psum_scatter(
        jnp.concatenate(
            [jnp.take(keys_acc, source, axis=0), jnp.take(values_acc, source, axis=0)], axis=1
        ),
        "blk",
        scatter_dimension=0,
        tiled=True,
    )
    key_grad = combined[:, :features].astype(jnp.bfloat16)
    value_grad = combined[:, features:].astype(jnp.bfloat16)
    return (query_total.astype(jnp.bfloat16), key_grad, value_grad)


MESH = pl.DeviceIdType.MESH
F32 = jnp.float32
BF16 = jnp.bfloat16


def mm(a, b, ca, cb):
    return lax.dot_general(a, b, (((ca,), (cb,)), ((), ())), preferred_element_type=F32)


def turn(x):
    return x.T


def fused(
    n_blk,
    n_grp,
    hd,
    q_ref,
    g_ref,
    k_ref,
    v_ref,
    order_ref,
    oq_ref,
    ok_ref,
    ov_ref,
    kv_in,
    kvt_own,
    kvt,
    qz,
    qgt_own,
    qgt,
    s_buf,
    d_buf,
    probs,
    qst,
    full_q,
    pair_st,
    pair_rv,
    own_st,
    full_kv,
    onehot,
    zst,
    l_s,
    kv_ss,
    kv_rs,
    fw_ss,
    fw_rs,
    z_ss,
    z_rs,
    q_ss,
    q_rs,
    b_ss,
    b_rs,
    p_ss,
    p_rs,
    d_ss,
    d_rs,
    o_ss,
    o_rs,
):
    b = lax.axis_index("blk")
    g = lax.axis_index("grp")
    chips = n_grp // 2
    p = g // 2
    c = g % 2
    partner = 2 * p + 1 - c
    rows = q_ref.shape[0]
    cols = k_ref.shape[0]
    gw = chips * hd
    scaling = 1.0 / math.sqrt(hd)
    expc = scaling * math.log2(math.e)

    def lanes(index, width):
        return pl.ds(pl.multiple_of(index * width, width), width)

    def describe(src, dst, ss, rs, bb, gg):
        return pltpu.make_async_remote_copy(
            src_ref=src,
            dst_ref=dst,
            send_sem=ss,
            recv_sem=rs,
            device_id=(bb, gg),
            device_id_type=MESH,
        )

    started = []

    def remote(*args):
        copy = describe(*args)
        copy.start()
        started.append(copy)
        return copy

    local = []
    for t, ref in enumerate((k_ref, v_ref)):
        local.append(pltpu.make_async_copy(ref.at[:, lanes(b, gw)], kv_in.at[t], l_s.at[t]))
    for t, ref in enumerate((q_ref, g_ref)):
        local.append(
            pltpu.make_async_copy(
                ref.at[:, lanes(b, gw)], qz.at[t, lanes(b, rows), :], l_s.at[2 + t]
            )
        )
    for copy in local:
        copy.start()

    barrier = pltpu.get_barrier_semaphore()
    for d in range(1, n_blk):
        pl.semaphore_signal(barrier, inc=1, device_id=((b + d) % n_blk, g), device_id_type=MESH)
    for e in range(1, chips):
        pl.semaphore_signal(
            barrier, inc=1, device_id=(b, 2 * ((p + e) % chips) + c), device_id_type=MESH
        )
    pl.semaphore_signal(barrier, inc=1, device_id=(b, partner), device_id_type=MESH)

    for t in range(2):
        local[t].wait()
        part = turn(kv_in[t])
        for hl in range(chips):
            kvt_own[hl, t] = part[hd * hl : hd * hl + hd]
    pl.semaphore_wait(barrier, n_blk + chips - 1)

    z_copies = {}
    for t, ref in enumerate((q_ref, g_ref)):
        for d in range(1, n_blk):
            bb = (b + d) % n_blk
            z_copies[t, d] = remote(
                ref.at[:, lanes(bb, gw)],
                qz.at[t, lanes(b, rows), :],
                z_ss.at[d - 1, t],
                z_rs.at[d - 1, t],
                bb,
                g,
            )
    kv_copies = {}
    for e in range(1, chips):
        pp = (p + e) % chips
        kv_copies[e] = remote(
            kvt_own.at[pp], kvt.at[g], kv_ss.at[e - 1], kv_rs.at[e - 1], b, 2 * pp + c
        )
    forwards = [remote(kvt_own.at[p], kvt.at[g], fw_ss.at[0], fw_rs.at[0], b, partner)]
    kvt[g] = kvt_own[p]

    row = lax.broadcasted_iota(jnp.int32, (PENCIL, cols), 0)
    col = lax.broadcasted_iota(jnp.int32, (PENCIL, cols), 1)
    per = rows // PENCIL
    for bb in range(n_blk):
        for k in range(per):
            first = order_ref[(bb * n_grp + g) * per + k] * PENCIL - g * cols
            onehot[pl.ds(bb * rows + k * PENCIL, PENCIL), :] = jnp.where(
                col - row == first, 1.0, 0.0
            ).astype(BF16)

    for t in range(2):
        local[2 + t].wait()
        for d in range(1, n_blk):
            z_copies[t, d].wait_recv()
        part = turn(qz[t])
        for hl in range(chips):
            qgt_own[hl, t] = part[hd * hl : hd * hl + hd]
        for e in range(1, chips):
            pp = (p + e) % chips
            remote(
                qgt_own.at[pp, t],
                qgt.at[p, t],
                q_ss.at[e - 1, t],
                q_rs.at[e - 1, t],
                b,
                2 * pp + c,
            )
        qgt[p, t] = qgt_own[p, t]
        if t == 0:
            for e in range(1, chips):
                src = 2 * ((p - e + chips) % chips) + c
                kv_copies[e].wait_recv()
                forwards.append(
                    remote(kvt.at[src], kvt.at[src], fw_ss.at[e], fw_rs.at[e], b, partner)
                )
    for copy in forwards:
        copy.wait_recv()

    def back(e, src):
        return describe(
            qst.at[e], full_q.at[p], b_ss.at[e - 1], b_rs.at[e - 1], b, 2 * src + c
        )

    def block(e, carry):
        src = (p - e + chips) % chips

        @pl.when(e > 0)
        def _():
            for t in range(2):
                describe(
                    qgt_own.at[0, t],
                    qgt.at[src, t],
                    q_ss.at[e - 1, t],
                    q_rs.at[e - 1, t],
                    b,
                    2 * src + c,
                ).wait_recv()

        qb = turn(qgt[src, 0])
        gb = turn(qgt[src, 1])
        top = jnp.full((cols, cols), -jnp.inf, F32)
        for n in range(n_grp):
            s = mm(qb, kvt[n, 0], 1, 0)
            s_buf[n] = s
            top = jnp.maximum(top, s)
        top = jnp.max(top, axis=1, keepdims=True)
        tot = jnp.zeros((cols, cols), F32)
        wtd = jnp.zeros((cols, cols), F32)
        for n in range(n_grp):
            x = jnp.exp2((s_buf[n] - top) * expc)
            dp = mm(gb, kvt[n, 1], 1, 0)
            s_buf[n] = x
            d_buf[n] = dp
            tot = tot + x
            wtd = wtd + x * dp
        inv = 1.0 / jnp.sum(tot, axis=1, keepdims=True)
        mean = jnp.sum(wtd, axis=1, keepdims=True) * inv
        acc = jnp.zeros((cols, hd), F32)
        for n in range(n_grp):
            soft = s_buf[n] * inv
            sg = (scaling * soft * (d_buf[n] - mean)).astype(BF16)
            probs[e, 0, n] = sg
            probs[e, 1, n] = soft.astype(BF16)
            acc = acc + mm(sg, kvt[n, 0], 1, 1)
        qst[e] = turn(acc).astype(BF16)

        @pl.when(e > 0)
        def _():
            back(e, src).start()

        return carry

    lax.fori_loop(0, chips, block, 0)
    full_q[p] = qst[0]

    def sums(t, n):
        total = mm(qgt[p, t], probs[0, t, n], 1, 0)
        for e in range(1, chips):
            total = total + mm(qgt[(p - e + chips) % chips, t], probs[e, t, n], 1, 0)
        return total

    order = [*range(1, chips), 0]
    pair = {}
    for t in range(2):
        for e in order:
            pair_st[e, t] = sums(t, 2 * ((p + e) % chips) + 1 - c).astype(BF16)
            pair[e, t] = remote(
                pair_st.at[e, t], pair_rv.at[e, t], p_ss.at[e, t], p_rs.at[e, t], b, partner
            )

    out_copies = []

    def deliver(t, value, out):
        zst[t] = value
        for d in range(1, n_blk):
            bb = (b + d) % n_blk
            out_copies.append(
                remote(
                    zst.at[t, lanes(bb, rows), :],
                    out.at[:, lanes(b, gw)],
                    o_ss.at[d - 1, t],
                    o_rs.at[d - 1, t],
                    bb,
                    g,
                )
            )
        out[:, lanes(b, gw)] = zst[t, lanes(b, rows), :]

    home = {}

    def finish(t):
        for e in order:
            pp = (p + e) % chips
            mine = sums(t, 2 * pp + c)
            pair[e, t].wait_recv()
            done = (mine + pair_rv[e, t].astype(F32)).astype(BF16)
            if e:
                own_st[e - 1, t] = done
                home[e, t] = remote(
                    own_st.at[e - 1, t],
                    full_kv.at[p, t],
                    d_ss.at[e - 1, t],
                    d_rs.at[e - 1, t],
                    b,
                    2 * pp + c,
                )
            else:
                full_kv[p, t] = done

    def permuted(t, out):
        for e in range(1, chips):
            home[e, t].wait_recv()
        both = full_kv[:, t].reshape(gw, cols)
        deliver(1 + t, mm(onehot[...], both, 1, 1).astype(BF16), out)

    finish(0)
    for e in range(1, chips):
        back(e, (p - e + chips) % chips).wait_recv()
    deliver(0, turn(full_q[...].reshape(gw, cols)), oq_ref)
    finish(1)
    permuted(0, ok_ref)
    permuted(1, ov_ref)

    for copy in out_copies:
        copy.wait_recv()
    for copy in started:
        copy.wait_send()
    for e in range(1, chips):
        back(e, (p - e + chips) % chips).wait_send()


def fused_on_device(n_blk, n_grp, obj_query, grad_out, pattern_key, pattern_value, pencil_order):
    rows, features = obj_query.shape
    cols = pattern_key.shape[0]
    hd = features // H
    chips = n_grp // 2
    gw = chips * hd
    dma = pltpu.SemaphoreType.DMA
    vmem = pl.BlockSpec(memory_space=pltpu.VMEM)
    anywhere = pl.BlockSpec(memory_space=pltpu.HBM)
    return tuple(
        pl.pallas_call(
            functools.partial(fused, n_blk, n_grp, hd),
            out_shape=[jax.ShapeDtypeStruct((rows, features), BF16)] * 3,
            in_specs=[anywhere] * 4 + [pl.BlockSpec(memory_space=pltpu.SMEM)],
            out_specs=[vmem] * 3,
            scratch_shapes=[
                pltpu.VMEM((2, cols, gw), BF16),
                pltpu.VMEM((chips, 2, hd, cols), BF16),
                pltpu.VMEM((n_grp, 2, hd, cols), BF16),
                pltpu.VMEM((2, cols, gw), BF16),
                pltpu.VMEM((chips, 2, hd, cols), BF16),
                pltpu.VMEM((chips, 2, hd, cols), BF16),
                pltpu.VMEM((n_grp, cols, cols), F32),
                pltpu.VMEM((n_grp, cols, cols), F32),
                pltpu.VMEM((chips, 2, n_grp, cols, cols), BF16),
                pltpu.VMEM((chips, hd, cols), BF16),
                pltpu.VMEM((chips, hd, cols), BF16),
                pltpu.VMEM((chips, 2, hd, cols), BF16),
                pltpu.VMEM((chips, 2, hd, cols), BF16),
                pltpu.VMEM((chips - 1, 2, hd, cols), BF16),
                pltpu.VMEM((chips, 2, hd, cols), BF16),
                pltpu.VMEM((cols, cols), BF16),
                pltpu.VMEM((3, cols, gw), BF16),
                dma((4,)),
                dma((chips - 1,)),
                dma((chips - 1,)),
                dma((chips,)),
                dma((chips,)),
                dma((n_blk - 1, 2)),
                dma((n_blk - 1, 2)),
                dma((chips - 1, 2)),
                dma((chips - 1, 2)),
                dma((chips - 1,)),
                dma((chips - 1,)),
                dma((chips, 2)),
                dma((chips, 2)),
                dma((chips - 1, 2)),
                dma((chips - 1, 2)),
                dma((n_blk - 1, 3)),
                dma((n_blk - 1, 3)),
            ],
            compiler_params=pltpu.CompilerParams(
                collective_id=0, has_side_effects=True, vmem_limit_bytes=56 * 1024 * 1024
            ),
        )(obj_query, grad_out, pattern_key, pattern_value, pencil_order)
    )


def solution(mesh):
    in_specs = (
        P(("blk", "grp"), None),
        P(("blk", "grp"), None),
        P("grp", None),
        P("grp", None),
        P(),
    )
    out_specs = (P(("blk", "grp"), None), P(("blk", "grp"), None), P(("blk", "grp"), None))
    n_blk, n_grp = mesh.shape["blk"], mesh.shape["grp"]

    def body(obj_query, grad_out, pattern_key, pattern_value, pencil_order):
        features = obj_query.shape[1]
        fits = (
            n_blk * n_grp // 2 == H
            and (features // n_blk) % 128 == 0
            and pattern_key.shape[0] == 256
            and n_blk * obj_query.shape[0] == 256
        )
        step = functools.partial(fused_on_device, n_blk, n_grp) if fits else on_device
        return step(obj_query, grad_out, pattern_key, pattern_value, pencil_order)

    return jax.shard_map(body, mesh=mesh, in_specs=in_specs, out_specs=out_specs, check_vma=False)
```

```python
import functools
import math

import jax
import jax.numpy as jnp
from jax import lax
from jax.experimental import pallas as pl
from jax.experimental.pallas import tpu as pltpu
from jax.sharding import PartitionSpec as P

H = 16
PENCIL = 16


def joined(value, axis, combine):
    everything = jax.tree.map(lambda part: lax.all_gather(part, axis), value)
    initial = jax.tree.map(lambda part: part[0], everything)

    def step(k, so_far):
        return combine(so_far, jax.tree.map(lambda part: part[k], everything))

    return lax.fori_loop(1, lax.axis_size(axis), step, initial)


def split_heads(matrix):
    return matrix.reshape(matrix.shape[0], H, matrix.shape[1] // H)


def block_stats(part_query, part_grad, key_block, value_block):
    scaling = 1.0 / math.sqrt(key_block.shape[1] // H)
    scores = (
        jnp.einsum(
            "rhd,chd->hrc",
            split_heads(part_query),
            split_heads(key_block),
            preferred_element_type=jnp.float32,
        )
        * scaling
    )
    prob_grad = jnp.einsum(
        "rhd,chd->hrc",
        split_heads(part_grad),
        split_heads(value_block),
        preferred_element_type=jnp.float32,
    )
    highest = jnp.max(scores, axis=2)
    weights = jnp.exp(scores - highest[:, :, None])
    return (highest, jnp.sum(weights, axis=2), jnp.sum(weights * prob_grad, axis=2))


def join_stats(earlier, later):
    highest = jnp.maximum(earlier[0], later[0])
    before = jnp.exp(earlier[0] - highest)
    after = jnp.exp(later[0] - highest)
    return (highest, earlier[1] * before + later[1] * after, earlier[2] * before + later[2] * after)


def stats_of_rows(queries, grads, key_block, value_block):
    amount, features = queries.shape
    blocking = math.gcd(amount, 128)

    def one_block(couple):
        return block_stats(couple[0], couple[1], key_block, value_block)

    stacked = lax.map(
        one_block,
        (
            queries.reshape(amount // blocking, blocking, features),
            grads.reshape(amount // blocking, blocking, features),
        ),
    )
    return tuple((jnp.moveaxis(member, 0, 1).reshape(H, amount) for member in stacked))


def block_grads(part_query, part_grad, log_now, mean_now, key_block, value_block):
    features = key_block.shape[1]
    scaling = 1.0 / math.sqrt(features // H)
    query_heads = split_heads(part_query)
    grad_heads = split_heads(part_grad)
    key_heads = split_heads(key_block)
    value_heads = split_heads(value_block)
    scores = (
        jnp.einsum("rhd,chd->hrc", query_heads, key_heads, preferred_element_type=jnp.float32)
        * scaling
    )
    prob_grad = jnp.einsum(
        "rhd,chd->hrc", grad_heads, value_heads, preferred_element_type=jnp.float32
    )
    softmax = jnp.exp(scores - log_now[:, :, None])
    softmax_low = softmax.astype(jnp.bfloat16)
    score_grad = (scaling * softmax * (prob_grad - mean_now[:, :, None])).astype(jnp.bfloat16)
    query_term = jnp.einsum(
        "hrc,chd->rhd", score_grad, key_heads, preferred_element_type=jnp.float32
    ).reshape(part_query.shape[0], features)
    key_term = jnp.einsum(
        "hrc,rhd->chd", score_grad, query_heads, preferred_element_type=jnp.float32
    ).reshape(key_block.shape[0], features)
    value_term = jnp.einsum(
        "hrc,rhd->chd", softmax_low, grad_heads, preferred_element_type=jnp.float32
    ).reshape(key_block.shape[0], features)
    return (query_term, key_term, value_term)


def on_device(obj_query, grad_out, pattern_key, pattern_value, pencil_order):
    amount, features = obj_query.shape
    columns = pattern_key.shape[0]
    groups = lax.axis_size("grp")
    position = lax.axis_index("grp")
    group_rows = groups * amount
    all_query, all_grad = (
        lax.all_gather(obj_query, "grp", axis=0, tiled=True),
        lax.all_gather(grad_out, "grp", axis=0, tiled=True),
    )
    partial_value = stats_of_rows(all_query, all_grad, pattern_key, pattern_value)
    highest, totals, weighted = joined(partial_value, "grp", join_stats)
    log_totals = highest + jnp.log(totals)
    mean_grads = weighted / totals
    blocking = math.gcd(group_rows, 128)
    sweeps = group_rows // blocking

    def sweep(carried, segment):
        keys_acc, values_acc = carried
        query_term, key_term, value_term = block_grads(
            segment[0], segment[1], segment[2], segment[3], pattern_key, pattern_value
        )
        return ((keys_acc + key_term, values_acc + value_term), query_term)

    log_blocks = jnp.moveaxis(log_totals.reshape(H, sweeps, blocking), 1, 0)
    mean_blocks = jnp.moveaxis(mean_grads.reshape(H, sweeps, blocking), 1, 0)
    zeros_acc = jnp.zeros((columns, features), jnp.float32)
    segments = (
        all_query.reshape(sweeps, blocking, features),
        all_grad.reshape(sweeps, blocking, features),
        log_blocks,
        mean_blocks,
    )
    (keys_acc, values_acc), pieces = lax.scan(sweep, (zeros_acc, zeros_acc), segments)
    query_total = lax.psum_scatter(
        pieces.reshape(group_rows, features), "grp", scatter_dimension=0, tiled=True
    )
    device_rows = columns // lax.axis_size("blk")
    spots = jnp.arange(columns, dtype=jnp.int32)
    target = (spots // device_rows * groups + position) * device_rows + spots % device_rows
    source = (
        jnp.take(pencil_order, target // PENCIL) * PENCIL + target % PENCIL - position * columns
    )
    combined = lax.psum_scatter(
        jnp.concatenate(
            [jnp.take(keys_acc, source, axis=0), jnp.take(values_acc, source, axis=0)], axis=1
        ),
        "blk",
        scatter_dimension=0,
        tiled=True,
    )
    key_grad = combined[:, :features].astype(jnp.bfloat16)
    value_grad = combined[:, features:].astype(jnp.bfloat16)
    return (query_total.astype(jnp.bfloat16), key_grad, value_grad)


MESH = pl.DeviceIdType.MESH
F32 = jnp.float32
BF16 = jnp.bfloat16


def mm(a, b, ca, cb):
    return lax.dot_general(a, b, (((ca,), (cb,)), ((), ())), preferred_element_type=F32)


def turn(x):
    return x.T


def fused(
    n_blk,
    n_grp,
    hd,
    q_ref,
    g_ref,
    k_ref,
    v_ref,
    order_ref,
    oq_ref,
    ok_ref,
    ov_ref,
    kv_in,
    kvt_own,
    kvt,
    qz,
    qgt_own,
    qgt,
    s_buf,
    d_buf,
    inv_buf,
    kvacc,
    qst,
    full_q,
    pair_st,
    pair_rv,
    own_st,
    full_kv,
    onehot,
    zst,
    l_s,
    kv_ss,
    kv_rs,
    fw_ss,
    fw_rs,
    z_ss,
    z_rs,
    q_ss,
    q_rs,
    b_ss,
    b_rs,
    p_ss,
    p_rs,
    d_ss,
    d_rs,
    o_ss,
    o_rs,
):
    b = lax.axis_index("blk")
    g = lax.axis_index("grp")
    chips = n_grp // 2
    p = g // 2
    c = g % 2
    partner = 2 * p + 1 - c
    rows = q_ref.shape[0]
    cols = k_ref.shape[0]
    gw = chips * hd
    scaling = 1.0 / math.sqrt(hd)
    expc = scaling * math.log2(math.e)

    def lanes(index, width):
        return pl.ds(pl.multiple_of(index * width, width), width)

    def describe(src, dst, ss, rs, bb, gg):
        return pltpu.make_async_remote_copy(
            src_ref=src,
            dst_ref=dst,
            send_sem=ss,
            recv_sem=rs,
            device_id=(bb, gg),
            device_id_type=MESH,
        )

    started = []

    def remote(*args):
        copy = describe(*args)
        copy.start()
        started.append(copy)
        return copy

    local = []
    for t, ref in enumerate((k_ref, v_ref)):
        local.append(pltpu.make_async_copy(ref.at[:, lanes(b, gw)], kv_in.at[t], l_s.at[t]))
    for t, ref in enumerate((q_ref, g_ref)):
        local.append(
            pltpu.make_async_copy(
                ref.at[:, lanes(b, gw)], qz.at[t, lanes(b, rows), :], l_s.at[2 + t]
            )
        )
    for copy in local:
        copy.start()

    barrier = pltpu.get_barrier_semaphore()
    for d in range(1, n_blk):
        pl.semaphore_signal(barrier, inc=1, device_id=((b + d) % n_blk, g), device_id_type=MESH)
    for e in range(1, chips):
        pl.semaphore_signal(
            barrier, inc=1, device_id=(b, 2 * ((p + e) % chips) + c), device_id_type=MESH
        )
    pl.semaphore_signal(barrier, inc=1, device_id=(b, partner), device_id_type=MESH)

    for t in range(2):
        local[t].wait()
        part = turn(kv_in[t])
        for hl in range(chips):
            kvt_own[hl, t] = part[hd * hl : hd * hl + hd]
    pl.semaphore_wait(barrier, n_blk + chips - 1)

    z_copies = {}
    kv_copies = {}
    forwards = {}
    for t, ref in enumerate((q_ref, g_ref)):
        for d in range(1, n_blk):
            bb = (b + d) % n_blk
            z_copies[t, d] = remote(
                ref.at[:, lanes(bb, gw)],
                qz.at[t, lanes(b, rows), :],
                z_ss.at[d - 1, t],
                z_rs.at[d - 1, t],
                bb,
                g,
            )
        for e in range(1, chips):
            pp = (p + e) % chips
            kv_copies[t, e] = remote(
                kvt_own.at[pp, t],
                kvt.at[g, t],
                kv_ss.at[e - 1, t],
                kv_rs.at[e - 1, t],
                b,
                2 * pp + c,
            )
        forwards[t, 0] = remote(
            kvt_own.at[p, t], kvt.at[g, t], fw_ss.at[0, t], fw_rs.at[0, t], b, partner
        )
    kvt[g] = kvt_own[p]
    kvacc[...] = jnp.zeros_like(kvacc)

    row = lax.broadcasted_iota(jnp.int32, (PENCIL, cols), 0)
    col = lax.broadcasted_iota(jnp.int32, (PENCIL, cols), 1)
    per = rows // PENCIL
    for bb in range(n_blk):
        for k in range(per):
            first = order_ref[(bb * n_grp + g) * per + k] * PENCIL - g * cols
            onehot[pl.ds(bb * rows + k * PENCIL, PENCIL), :] = jnp.where(
                col - row == first, 1.0, 0.0
            ).astype(BF16)

    def forward(t):
        for e in range(1, chips):
            src = 2 * ((p - e + chips) % chips) + c
            kv_copies[t, e].wait_recv()
            forwards[t, e] = remote(
                kvt.at[src, t], kvt.at[src, t], fw_ss.at[e, t], fw_rs.at[e, t], b, partner
            )

    def exchange(t):
        local[2 + t].wait()
        for d in range(1, n_blk):
            z_copies[t, d].wait_recv()
        part = turn(qz[t])
        for hl in range(chips):
            qgt_own[hl, t] = part[hd * hl : hd * hl + hd]
        for e in range(1, chips):
            pp = (p + e) % chips
            remote(
                qgt_own.at[pp, t],
                qgt.at[p, t],
                q_ss.at[e - 1, t],
                q_rs.at[e - 1, t],
                b,
                2 * pp + c,
            )
        qgt[p, t] = qgt_own[p, t]

    def arrived(t, e, src):
        describe(
            qgt_own.at[0, t],
            qgt.at[src, t],
            q_ss.at[e - 1, t],
            q_rs.at[e - 1, t],
            b,
            2 * src + c,
        ).wait_recv()

    def from_chip(e):
        return (p - e + chips) % chips

    def back(e, src):
        return describe(
            qst.at[e], full_q.at[p], b_ss.at[e - 1], b_rs.at[e - 1], b, 2 * src + c
        )

    def weights(e, carry):
        src = from_chip(e)

        @pl.when(e > 0)
        def _():
            arrived(0, e, src)

        qb = turn(qgt[src, 0])
        top = jnp.full((cols, cols), -jnp.inf, F32)
        for n in range(n_grp):
            s = mm(qb, kvt[n, 0], 1, 0)
            s_buf[e, n] = s
            top = jnp.maximum(top, s)
        top = jnp.max(top, axis=1, keepdims=True)
        tot = jnp.zeros((cols, cols), F32)
        for n in range(n_grp):
            x = jnp.exp2((s_buf[e, n] - top) * expc)
            s_buf[e, n] = x
            tot = tot + x
        inv_buf[e] = 1.0 / jnp.sum(tot, axis=1, keepdims=True)
        return carry

    def value_sums(n):
        total = jnp.zeros((hd, cols), F32)
        for e in range(chips):
            low = (s_buf[e, n] * inv_buf[e]).astype(BF16)
            total = total + mm(qgt[from_chip(e), 1], low, 1, 0)
        return total

    def grads(e, carry):
        src = from_chip(e)
        qt = qgt[src, 0]
        gb = turn(qgt[src, 1])
        wtd = jnp.zeros((cols, cols), F32)
        for n in range(n_grp):
            dp = mm(gb, kvt[n, 1], 1, 0)
            d_buf[n] = dp
            wtd = wtd + s_buf[e, n] * dp
        inv = inv_buf[e]
        mean = jnp.sum(wtd, axis=1, keepdims=True) * inv
        acc = jnp.zeros((cols, hd), F32)
        for n in range(n_grp):
            soft = s_buf[e, n] * inv
            sg = (scaling * soft * (d_buf[n] - mean)).astype(BF16)
            kvacc[0, n] += mm(qt, sg, 1, 0)
            acc = acc + mm(sg, kvt[n, 0], 1, 1)
        qst[e] = turn(acc).astype(BF16)

        @pl.when(e > 0)
        def _():
            back(e, src).start()

        return carry

    order = [*range(1, chips), 0]
    pair = {}

    def swap(t, e, total):
        pair_st[e, t] = total.astype(BF16)
        pair[e, t] = remote(
            pair_st.at[e, t], pair_rv.at[e, t], p_ss.at[e, t], p_rs.at[e, t], b, partner
        )

    forward(0)
    exchange(0)
    for e in range(chips):
        forwards[0, e].wait_recv()
    lax.fori_loop(0, 2, weights, 0)
    forward(1)
    exchange(1)
    lax.fori_loop(2, chips, weights, 0)
    for e in range(1, chips):
        arrived(1, e, from_chip(e))
    for e in order:
        swap(1, e, value_sums(2 * ((p + e) % chips) + 1 - c))
    for e in order:
        n = 2 * ((p + e) % chips) + c
        kvacc[1, n] = value_sums(n)
    for e in range(chips):
        forwards[1, e].wait_recv()
    lax.fori_loop(0, 2, grads, 0)

    out_copies = []

    def deliver(t, value, out):
        zst[t] = value
        for d in range(1, n_blk):
            bb = (b + d) % n_blk
            out_copies.append(
                remote(
                    zst.at[t, lanes(bb, rows), :],
                    out.at[:, lanes(b, gw)],
                    o_ss.at[d - 1, t],
                    o_rs.at[d - 1, t],
                    bb,
                    g,
                )
            )
        out[:, lanes(b, gw)] = zst[t, lanes(b, rows), :]

    home = {}

    def finish(t):
        for e in order:
            pp = (p + e) % chips
            mine = kvacc[t, 2 * pp + c]
            pair[e, t].wait_recv()
            done = (mine + pair_rv[e, t].astype(F32)).astype(BF16)
            if e:
                own_st[e - 1, t] = done
                home[e, t] = remote(
                    own_st.at[e - 1, t],
                    full_kv.at[p, t],
                    d_ss.at[e - 1, t],
                    d_rs.at[e - 1, t],
                    b,
                    2 * pp + c,
                )
            else:
                full_kv[p, t] = done

    def permuted(t, out):
        for e in range(1, chips):
            home[e, t].wait_recv()
        both = full_kv[:, t].reshape(gw, cols)
        deliver(1 + t, mm(onehot[...], both, 1, 1).astype(BF16), out)

    finish(1)
    lax.fori_loop(2, chips, grads, 0)
    full_q[p] = qst[0]
    for e in order:
        swap(0, e, kvacc[0, 2 * ((p + e) % chips) + 1 - c])
    permuted(1, ov_ref)
    for e in range(1, chips):
        back(e, from_chip(e)).wait_recv()
    deliver(0, turn(full_q[...].reshape(gw, cols)), oq_ref)
    finish(0)
    permuted(0, ok_ref)

    for copy in out_copies:
        copy.wait_recv()
    for copy in started:
        copy.wait_send()
    for e in range(1, chips):
        back(e, from_chip(e)).wait_send()


def fused_on_device(n_blk, n_grp, obj_query, grad_out, pattern_key, pattern_value, pencil_order):
    rows, features = obj_query.shape
    cols = pattern_key.shape[0]
    hd = features // H
    chips = n_grp // 2
    gw = chips * hd
    dma = pltpu.SemaphoreType.DMA
    vmem = pl.BlockSpec(memory_space=pltpu.VMEM)
    anywhere = pl.BlockSpec(memory_space=pltpu.HBM)
    return tuple(
        pl.pallas_call(
            functools.partial(fused, n_blk, n_grp, hd),
            out_shape=[jax.ShapeDtypeStruct((rows, features), BF16)] * 3,
            in_specs=[anywhere] * 4 + [pl.BlockSpec(memory_space=pltpu.SMEM)],
            out_specs=[vmem] * 3,
            scratch_shapes=[
                pltpu.VMEM((2, cols, gw), BF16),
                pltpu.VMEM((chips, 2, hd, cols), BF16),
                pltpu.VMEM((n_grp, 2, hd, cols), BF16),
                pltpu.VMEM((2, cols, gw), BF16),
                pltpu.VMEM((chips, 2, hd, cols), BF16),
                pltpu.VMEM((chips, 2, hd, cols), BF16),
                pltpu.VMEM((chips, n_grp, cols, cols), F32),
                pltpu.VMEM((n_grp, cols, cols), F32),
                pltpu.VMEM((chips, cols, 1), F32),
                pltpu.VMEM((2, n_grp, hd, cols), F32),
                pltpu.VMEM((chips, hd, cols), BF16),
                pltpu.VMEM((chips, hd, cols), BF16),
                pltpu.VMEM((chips, 2, hd, cols), BF16),
                pltpu.VMEM((chips, 2, hd, cols), BF16),
                pltpu.VMEM((chips - 1, 2, hd, cols), BF16),
                pltpu.VMEM((chips, 2, hd, cols), BF16),
                pltpu.VMEM((cols, cols), BF16),
                pltpu.VMEM((3, cols, gw), BF16),
                dma((4,)),
                dma((chips - 1, 2)),
                dma((chips - 1, 2)),
                dma((chips, 2)),
                dma((chips, 2)),
                dma((n_blk - 1, 2)),
                dma((n_blk - 1, 2)),
                dma((chips - 1, 2)),
                dma((chips - 1, 2)),
                dma((chips - 1,)),
                dma((chips - 1,)),
                dma((chips, 2)),
                dma((chips, 2)),
                dma((chips - 1, 2)),
                dma((chips - 1, 2)),
                dma((n_blk - 1, 3)),
                dma((n_blk - 1, 3)),
            ],
            compiler_params=pltpu.CompilerParams(
                collective_id=0, has_side_effects=True, vmem_limit_bytes=56 * 1024 * 1024
            ),
        )(obj_query, grad_out, pattern_key, pattern_value, pencil_order)
    )


def solution(mesh):
    in_specs = (
        P(("blk", "grp"), None),
        P(("blk", "grp"), None),
        P("grp", None),
        P("grp", None),
        P(),
    )
    out_specs = (P(("blk", "grp"), None), P(("blk", "grp"), None), P(("blk", "grp"), None))
    n_blk, n_grp = mesh.shape["blk"], mesh.shape["grp"]

    def body(obj_query, grad_out, pattern_key, pattern_value, pencil_order):
        features = obj_query.shape[1]
        fits = (
            n_blk * n_grp // 2 == H
            and (features // n_blk) % 128 == 0
            and pattern_key.shape[0] == 256
            and n_blk * obj_query.shape[0] == 256
        )
        step = functools.partial(fused_on_device, n_blk, n_grp) if fits else on_device
        return step(obj_query, grad_out, pattern_key, pattern_value, pencil_order)

    return jax.shard_map(body, mesh=mesh, in_specs=in_specs, out_specs=out_specs, check_vma=False)
```

```python
import functools
import math

import jax
import jax.numpy as jnp
from jax import lax
from jax.experimental import pallas as pl
from jax.experimental.pallas import tpu as pltpu
from jax.sharding import PartitionSpec as P

H = 16
PENCIL = 16


def joined(value, axis, combine):
    everything = jax.tree.map(lambda part: lax.all_gather(part, axis), value)
    initial = jax.tree.map(lambda part: part[0], everything)

    def step(k, so_far):
        return combine(so_far, jax.tree.map(lambda part: part[k], everything))

    return lax.fori_loop(1, lax.axis_size(axis), step, initial)


def split_heads(matrix):
    return matrix.reshape(matrix.shape[0], H, matrix.shape[1] // H)


def block_stats(part_query, part_grad, key_block, value_block):
    scaling = 1.0 / math.sqrt(key_block.shape[1] // H)
    scores = (
        jnp.einsum(
            "rhd,chd->hrc",
            split_heads(part_query),
            split_heads(key_block),
            preferred_element_type=jnp.float32,
        )
        * scaling
    )
    prob_grad = jnp.einsum(
        "rhd,chd->hrc",
        split_heads(part_grad),
        split_heads(value_block),
        preferred_element_type=jnp.float32,
    )
    highest = jnp.max(scores, axis=2)
    weights = jnp.exp(scores - highest[:, :, None])
    return (highest, jnp.sum(weights, axis=2), jnp.sum(weights * prob_grad, axis=2))


def join_stats(earlier, later):
    highest = jnp.maximum(earlier[0], later[0])
    before = jnp.exp(earlier[0] - highest)
    after = jnp.exp(later[0] - highest)
    return (highest, earlier[1] * before + later[1] * after, earlier[2] * before + later[2] * after)


def stats_of_rows(queries, grads, key_block, value_block):
    amount, features = queries.shape
    blocking = math.gcd(amount, 128)

    def one_block(couple):
        return block_stats(couple[0], couple[1], key_block, value_block)

    stacked = lax.map(
        one_block,
        (
            queries.reshape(amount // blocking, blocking, features),
            grads.reshape(amount // blocking, blocking, features),
        ),
    )
    return tuple((jnp.moveaxis(member, 0, 1).reshape(H, amount) for member in stacked))


def block_grads(part_query, part_grad, log_now, mean_now, key_block, value_block):
    features = key_block.shape[1]
    scaling = 1.0 / math.sqrt(features // H)
    query_heads = split_heads(part_query)
    grad_heads = split_heads(part_grad)
    key_heads = split_heads(key_block)
    value_heads = split_heads(value_block)
    scores = (
        jnp.einsum("rhd,chd->hrc", query_heads, key_heads, preferred_element_type=jnp.float32)
        * scaling
    )
    prob_grad = jnp.einsum(
        "rhd,chd->hrc", grad_heads, value_heads, preferred_element_type=jnp.float32
    )
    softmax = jnp.exp(scores - log_now[:, :, None])
    softmax_low = softmax.astype(jnp.bfloat16)
    score_grad = (scaling * softmax * (prob_grad - mean_now[:, :, None])).astype(jnp.bfloat16)
    query_term = jnp.einsum(
        "hrc,chd->rhd", score_grad, key_heads, preferred_element_type=jnp.float32
    ).reshape(part_query.shape[0], features)
    key_term = jnp.einsum(
        "hrc,rhd->chd", score_grad, query_heads, preferred_element_type=jnp.float32
    ).reshape(key_block.shape[0], features)
    value_term = jnp.einsum(
        "hrc,rhd->chd", softmax_low, grad_heads, preferred_element_type=jnp.float32
    ).reshape(key_block.shape[0], features)
    return (query_term, key_term, value_term)


def on_device(obj_query, grad_out, pattern_key, pattern_value, pencil_order):
    amount, features = obj_query.shape
    columns = pattern_key.shape[0]
    groups = lax.axis_size("grp")
    position = lax.axis_index("grp")
    group_rows = groups * amount
    all_query, all_grad = (
        lax.all_gather(obj_query, "grp", axis=0, tiled=True),
        lax.all_gather(grad_out, "grp", axis=0, tiled=True),
    )
    partial_value = stats_of_rows(all_query, all_grad, pattern_key, pattern_value)
    highest, totals, weighted = joined(partial_value, "grp", join_stats)
    log_totals = highest + jnp.log(totals)
    mean_grads = weighted / totals
    blocking = math.gcd(group_rows, 128)
    sweeps = group_rows // blocking

    def sweep(carried, segment):
        keys_acc, values_acc = carried
        query_term, key_term, value_term = block_grads(
            segment[0], segment[1], segment[2], segment[3], pattern_key, pattern_value
        )
        return ((keys_acc + key_term, values_acc + value_term), query_term)

    log_blocks = jnp.moveaxis(log_totals.reshape(H, sweeps, blocking), 1, 0)
    mean_blocks = jnp.moveaxis(mean_grads.reshape(H, sweeps, blocking), 1, 0)
    zeros_acc = jnp.zeros((columns, features), jnp.float32)
    segments = (
        all_query.reshape(sweeps, blocking, features),
        all_grad.reshape(sweeps, blocking, features),
        log_blocks,
        mean_blocks,
    )
    (keys_acc, values_acc), pieces = lax.scan(sweep, (zeros_acc, zeros_acc), segments)
    query_total = lax.psum_scatter(
        pieces.reshape(group_rows, features), "grp", scatter_dimension=0, tiled=True
    )
    device_rows = columns // lax.axis_size("blk")
    spots = jnp.arange(columns, dtype=jnp.int32)
    target = (spots // device_rows * groups + position) * device_rows + spots % device_rows
    source = (
        jnp.take(pencil_order, target // PENCIL) * PENCIL + target % PENCIL - position * columns
    )
    combined = lax.psum_scatter(
        jnp.concatenate(
            [jnp.take(keys_acc, source, axis=0), jnp.take(values_acc, source, axis=0)], axis=1
        ),
        "blk",
        scatter_dimension=0,
        tiled=True,
    )
    key_grad = combined[:, :features].astype(jnp.bfloat16)
    value_grad = combined[:, features:].astype(jnp.bfloat16)
    return (query_total.astype(jnp.bfloat16), key_grad, value_grad)


MESH = pl.DeviceIdType.MESH
F32 = jnp.float32
BF16 = jnp.bfloat16


def mm(a, b, ca, cb):
    return lax.dot_general(a, b, (((ca,), (cb,)), ((), ())), preferred_element_type=F32)


def turn(x):
    return x.T


def fused(
    n_blk,
    n_grp,
    hd,
    q_ref,
    g_ref,
    k_ref,
    v_ref,
    order_ref,
    out_ref,
    kv_in,
    kvt_own,
    kvt,
    qz,
    qgt_own,
    qgt,
    s_buf,
    d_buf,
    inv_buf,
    probs,
    own_v,
    qst,
    full_q,
    pair_st,
    pair_rv,
    own_st,
    full_kv,
    onehot,
    zst,
    l_s,
    kv_ss,
    kv_rs,
    fw_ss,
    fw_rs,
    z_ss,
    z_rs,
    q_ss,
    q_rs,
    b_ss,
    b_rs,
    p_ss,
    p_rs,
    d_ss,
    d_rs,
    o_ss,
    o_rs,
):
    b = lax.axis_index("blk")
    g = lax.axis_index("grp")
    chips = n_grp // 2
    p = g // 2
    c = g % 2
    partner = 2 * p + 1 - c
    rows = q_ref.shape[0]
    cols = k_ref.shape[0]
    gw = chips * hd
    scaling = 1.0 / math.sqrt(hd)
    expc = scaling * math.log2(math.e)

    def lanes(index, width):
        return pl.ds(pl.multiple_of(index * width, width), width)

    def describe(src, dst, ss, rs, bb, gg):
        return pltpu.make_async_remote_copy(
            src_ref=src,
            dst_ref=dst,
            send_sem=ss,
            recv_sem=rs,
            device_id=(bb, gg),
            device_id_type=MESH,
        )

    started = []

    def remote(*args):
        copy = describe(*args)
        copy.start()
        started.append(copy)
        return copy

    local = []
    for t, ref in enumerate((k_ref, v_ref)):
        local.append(pltpu.make_async_copy(ref.at[:, lanes(b, gw)], kv_in.at[t], l_s.at[t]))
    for t, ref in enumerate((q_ref, g_ref)):
        local.append(
            pltpu.make_async_copy(
                ref.at[:, lanes(b, gw)], qz.at[t, lanes(b, rows), :], l_s.at[2 + t]
            )
        )
    for copy in local:
        copy.start()

    barrier = pltpu.get_barrier_semaphore()
    for d in range(1, n_blk):
        pl.semaphore_signal(barrier, inc=1, device_id=((b + d) % n_blk, g), device_id_type=MESH)
    for e in range(1, chips):
        pl.semaphore_signal(
            barrier, inc=1, device_id=(b, 2 * ((p + e) % chips) + c), device_id_type=MESH
        )
    pl.semaphore_signal(barrier, inc=1, device_id=(b, partner), device_id_type=MESH)

    pl.semaphore_wait(barrier, n_blk + chips - 1)

    z_copies = {}
    kv_copies = {}
    forwards = {}
    for t, ref in enumerate((q_ref, g_ref)):
        for d in range(1, n_blk):
            bb = (b + d) % n_blk
            z_copies[t, d] = remote(
                ref.at[:, lanes(bb, gw)],
                qz.at[t, lanes(b, rows), :],
                z_ss.at[d - 1, t],
                z_rs.at[d - 1, t],
                bb,
                g,
            )
    for t in range(2):
        local[t].wait()
        part = turn(kv_in[t])
        for hl in range(chips):
            kvt_own[hl, t] = part[hd * hl : hd * hl + hd]
        for e in range(1, chips):
            pp = (p + e) % chips
            kv_copies[t, e] = remote(
                kvt_own.at[pp, t],
                kvt.at[g, t],
                kv_ss.at[e - 1, t],
                kv_rs.at[e - 1, t],
                b,
                2 * pp + c,
            )
        forwards[t, 0] = remote(
            kvt_own.at[p, t], kvt.at[g, t], fw_ss.at[0, t], fw_rs.at[0, t], b, partner
        )
    kvt[g] = kvt_own[p]

    row = lax.broadcasted_iota(jnp.int32, (PENCIL, cols), 0)
    col = lax.broadcasted_iota(jnp.int32, (PENCIL, cols), 1)
    per = rows // PENCIL
    for bb in range(n_blk):
        for k in range(per):
            first = order_ref[(bb * n_grp + g) * per + k] * PENCIL - g * cols
            onehot[pl.ds(bb * rows + k * PENCIL, PENCIL), :] = jnp.where(
                col - row == first, 1.0, 0.0
            ).astype(BF16)

    def forward(t):
        for e in range(1, chips):
            src = 2 * ((p - e + chips) % chips) + c
            kv_copies[t, e].wait_recv()
            forwards[t, e] = remote(
                kvt.at[src, t], kvt.at[src, t], fw_ss.at[e, t], fw_rs.at[e, t], b, partner
            )

    def exchange(t):
        local[2 + t].wait()
        for d in range(1, n_blk):
            z_copies[t, d].wait_recv()
        part = turn(qz[t])
        for hl in range(chips):
            qgt_own[hl, t] = part[hd * hl : hd * hl + hd]
        for e in range(1, chips):
            pp = (p + e) % chips
            remote(
                qgt_own.at[pp, t],
                qgt.at[p, t],
                q_ss.at[e - 1, t],
                q_rs.at[e - 1, t],
                b,
                2 * pp + c,
            )
        qgt[p, t] = qgt_own[p, t]

    def arrived(t, e, src):
        describe(
            qgt_own.at[0, t],
            qgt.at[src, t],
            q_ss.at[e - 1, t],
            q_rs.at[e - 1, t],
            b,
            2 * src + c,
        ).wait_recv()

    def from_chip(e):
        return (p - e + chips) % chips

    def back(e, src):
        return describe(
            qst.at[e], full_q.at[p], b_ss.at[e - 1], b_rs.at[e - 1], b, 2 * src + c
        )

    def weights(e, carry):
        src = from_chip(e)

        @pl.when(e > 0)
        def _():
            arrived(0, e, src)

        qb = turn(qgt[src, 0])
        top = jnp.full((cols, cols), -jnp.inf, F32)
        for n in range(n_grp):
            s = mm(qb, kvt[n, 0], 1, 0)
            s_buf[e, n] = s
            top = jnp.maximum(top, s)
        top = jnp.max(top, axis=1, keepdims=True)
        tot = jnp.zeros((cols, cols), F32)
        for n in range(n_grp):
            x = jnp.exp2((s_buf[e, n] - top) * expc)
            s_buf[e, n] = x
            tot = tot + x
        inv_buf[e] = 1.0 / jnp.sum(tot, axis=1, keepdims=True)
        return carry

    def value_sums(n):
        total = jnp.zeros((hd, cols), F32)
        for e in range(chips):
            low = (s_buf[e, n] * inv_buf[e]).astype(BF16)
            total = total + mm(qgt[from_chip(e), 1], low, 1, 0)
        return total

    def key_sums(n):
        total = jnp.zeros((hd, cols), F32)
        for e in range(chips):
            total = total + mm(qgt[from_chip(e), 0], probs[e, n], 1, 0)
        return total

    def grads(e, carry):
        src = from_chip(e)
        gb = turn(qgt[src, 1])
        wtd = jnp.zeros((cols, cols), F32)
        for n in range(n_grp):
            dp = mm(gb, kvt[n, 1], 1, 0)
            d_buf[n] = dp
            wtd = wtd + s_buf[e, n] * dp
        inv = inv_buf[e]
        mean = jnp.sum(wtd, axis=1, keepdims=True) * inv
        acc = jnp.zeros((cols, hd), F32)
        for n in range(n_grp):
            soft = s_buf[e, n] * inv
            sg = (scaling * soft * (d_buf[n] - mean)).astype(BF16)
            probs[e, n] = sg
            acc = acc + mm(sg, kvt[n, 0], 1, 1)
        qst[e] = turn(acc).astype(BF16)

        @pl.when(e > 0)
        def _():
            back(e, src).start()

        return carry

    order = [*range(1, chips), 0]
    pair = {}

    def swap(t, e, total):
        pair_st[e, t] = total.astype(BF16)
        pair[e, t] = remote(
            pair_st.at[e, t], pair_rv.at[e, t], p_ss.at[e, t], p_rs.at[e, t], b, partner
        )

    forward(0)
    exchange(0)
    for e in range(chips):
        forwards[0, e].wait_recv()
    lax.fori_loop(0, 2, weights, 0)
    forward(1)
    exchange(1)
    lax.fori_loop(2, chips, weights, 0)
    for e in range(1, chips):
        arrived(1, e, from_chip(e))
    for e in order:
        swap(1, e, value_sums(2 * ((p + e) % chips) + 1 - c))
    for e in order:
        own_v[e] = value_sums(2 * ((p + e) % chips) + c)
    for e in range(chips):
        forwards[1, e].wait_recv()

    out_copies = []

    def deliver(t, value):
        zst[t] = value
        for d in range(1, n_blk):
            bb = (b + d) % n_blk
            out_copies.append(
                remote(
                    zst.at[t, lanes(bb, rows), :],
                    out_ref.at[t, :, lanes(b, gw)],
                    o_ss.at[d - 1, t],
                    o_rs.at[d - 1, t],
                    bb,
                    g,
                )
            )
        out_ref[t, :, lanes(b, gw)] = zst[t, lanes(b, rows), :]

    home = {}

    def finish(t):
        for e in order:
            pp = (p + e) % chips
            mine = own_v[e] if t else key_sums(2 * pp + c)
            pair[e, t].wait_recv()
            done = (mine + pair_rv[e, t].astype(F32)).astype(BF16)
            if e:
                own_st[e - 1, t] = done
                home[e, t] = remote(
                    own_st.at[e - 1, t],
                    full_kv.at[p, t],
                    d_ss.at[e - 1, t],
                    d_rs.at[e - 1, t],
                    b,
                    2 * pp + c,
                )
            else:
                full_kv[p, t] = done

    def permuted(t):
        for e in range(1, chips):
            home[e, t].wait_recv()
        both = full_kv[:, t].reshape(gw, cols)
        deliver(1 + t, mm(onehot[...], both, 1, 1).astype(BF16))

    finish(1)
    lax.fori_loop(0, 2, grads, 0)
    permuted(1)
    lax.fori_loop(2, chips, grads, 0)
    full_q[p] = qst[0]
    for e in order:
        swap(0, e, key_sums(2 * ((p + e) % chips) + 1 - c))
    for e in range(1, chips):
        back(e, from_chip(e)).wait_recv()
    deliver(0, turn(full_q[...].reshape(gw, cols)))
    finish(0)
    permuted(0)

    for copy in out_copies:
        copy.wait_recv()
    for copy in started:
        copy.wait_send()
    for e in range(1, chips):
        back(e, from_chip(e)).wait_send()


def fused_on_device(n_blk, n_grp, obj_query, grad_out, pattern_key, pattern_value, pencil_order):
    rows, features = obj_query.shape
    cols = pattern_key.shape[0]
    hd = features // H
    chips = n_grp // 2
    gw = chips * hd
    dma = pltpu.SemaphoreType.DMA
    vmem = pl.BlockSpec(memory_space=pltpu.VMEM)
    anywhere = pl.BlockSpec(memory_space=pltpu.HBM)
    joined_out = (
        pl.pallas_call(
            functools.partial(fused, n_blk, n_grp, hd),
            out_shape=jax.ShapeDtypeStruct((3, rows, features), BF16),
            in_specs=[anywhere] * 4 + [pl.BlockSpec(memory_space=pltpu.SMEM)],
            out_specs=vmem,
            scratch_shapes=[
                pltpu.VMEM((2, cols, gw), BF16),
                pltpu.VMEM((chips, 2, hd, cols), BF16),
                pltpu.VMEM((n_grp, 2, hd, cols), BF16),
                pltpu.VMEM((2, cols, gw), BF16),
                pltpu.VMEM((chips, 2, hd, cols), BF16),
                pltpu.VMEM((chips, 2, hd, cols), BF16),
                pltpu.VMEM((chips, n_grp, cols, cols), F32),
                pltpu.VMEM((n_grp, cols, cols), F32),
                pltpu.VMEM((chips, cols, 1), F32),
                pltpu.VMEM((chips, n_grp, cols, cols), BF16),
                pltpu.VMEM((chips, hd, cols), F32),
                pltpu.VMEM((chips, hd, cols), BF16),
                pltpu.VMEM((chips, hd, cols), BF16),
                pltpu.VMEM((chips, 2, hd, cols), BF16),
                pltpu.VMEM((chips, 2, hd, cols), BF16),
                pltpu.VMEM((chips - 1, 2, hd, cols), BF16),
                pltpu.VMEM((chips, 2, hd, cols), BF16),
                pltpu.VMEM((cols, cols), BF16),
                pltpu.VMEM((3, cols, gw), BF16),
                dma((4,)),
                dma((chips - 1, 2)),
                dma((chips - 1, 2)),
                dma((chips, 2)),
                dma((chips, 2)),
                dma((n_blk - 1, 2)),
                dma((n_blk - 1, 2)),
                dma((chips - 1, 2)),
                dma((chips - 1, 2)),
                dma((chips - 1,)),
                dma((chips - 1,)),
                dma((chips, 2)),
                dma((chips, 2)),
                dma((chips - 1, 2)),
                dma((chips - 1, 2)),
                dma((n_blk - 1, 3)),
                dma((n_blk - 1, 3)),
            ],
            compiler_params=pltpu.CompilerParams(
                collective_id=0, has_side_effects=True, vmem_limit_bytes=56 * 1024 * 1024
            ),
        )(obj_query, grad_out, pattern_key, pattern_value, pencil_order)
    )
    return joined_out[0], joined_out[1], joined_out[2]


def solution(mesh):
    in_specs = (
        P(("blk", "grp"), None),
        P(("blk", "grp"), None),
        P("grp", None),
        P("grp", None),
        P(),
    )
    out_specs = (P(("blk", "grp"), None), P(("blk", "grp"), None), P(("blk", "grp"), None))
    n_blk, n_grp = mesh.shape["blk"], mesh.shape["grp"]

    def body(obj_query, grad_out, pattern_key, pattern_value, pencil_order):
        features = obj_query.shape[1]
        fits = (
            n_blk * n_grp // 2 == H
            and (features // n_blk) % 128 == 0
            and pattern_key.shape[0] == 256
            and n_blk * obj_query.shape[0] == 256
        )
        step = functools.partial(fused_on_device, n_blk, n_grp) if fits else on_device
        return step(obj_query, grad_out, pattern_key, pattern_value, pencil_order)

    return jax.shard_map(body, mesh=mesh, in_specs=in_specs, out_specs=out_specs, check_vma=False)
```

```python
import functools
import math

import jax
import jax.numpy as jnp
from jax import lax
from jax.experimental import pallas as pl
from jax.experimental.pallas import tpu as pltpu
from jax.sharding import PartitionSpec as P

H = 16
PENCIL = 16


def joined(value, axis, combine):
    everything = jax.tree.map(lambda part: lax.all_gather(part, axis), value)
    initial = jax.tree.map(lambda part: part[0], everything)

    def step(k, so_far):
        return combine(so_far, jax.tree.map(lambda part: part[k], everything))

    return lax.fori_loop(1, lax.axis_size(axis), step, initial)


def split_heads(matrix):
    return matrix.reshape(matrix.shape[0], H, matrix.shape[1] // H)


def block_stats(part_query, part_grad, key_block, value_block):
    scaling = 1.0 / math.sqrt(key_block.shape[1] // H)
    scores = (
        jnp.einsum(
            "rhd,chd->hrc",
            split_heads(part_query),
            split_heads(key_block),
            preferred_element_type=jnp.float32,
        )
        * scaling
    )
    prob_grad = jnp.einsum(
        "rhd,chd->hrc",
        split_heads(part_grad),
        split_heads(value_block),
        preferred_element_type=jnp.float32,
    )
    highest = jnp.max(scores, axis=2)
    weights = jnp.exp(scores - highest[:, :, None])
    return (highest, jnp.sum(weights, axis=2), jnp.sum(weights * prob_grad, axis=2))


def join_stats(earlier, later):
    highest = jnp.maximum(earlier[0], later[0])
    before = jnp.exp(earlier[0] - highest)
    after = jnp.exp(later[0] - highest)
    return (highest, earlier[1] * before + later[1] * after, earlier[2] * before + later[2] * after)


def stats_of_rows(queries, grads, key_block, value_block):
    amount, features = queries.shape
    blocking = math.gcd(amount, 128)

    def one_block(couple):
        return block_stats(couple[0], couple[1], key_block, value_block)

    stacked = lax.map(
        one_block,
        (
            queries.reshape(amount // blocking, blocking, features),
            grads.reshape(amount // blocking, blocking, features),
        ),
    )
    return tuple((jnp.moveaxis(member, 0, 1).reshape(H, amount) for member in stacked))


def block_grads(part_query, part_grad, log_now, mean_now, key_block, value_block):
    features = key_block.shape[1]
    scaling = 1.0 / math.sqrt(features // H)
    query_heads = split_heads(part_query)
    grad_heads = split_heads(part_grad)
    key_heads = split_heads(key_block)
    value_heads = split_heads(value_block)
    scores = (
        jnp.einsum("rhd,chd->hrc", query_heads, key_heads, preferred_element_type=jnp.float32)
        * scaling
    )
    prob_grad = jnp.einsum(
        "rhd,chd->hrc", grad_heads, value_heads, preferred_element_type=jnp.float32
    )
    softmax = jnp.exp(scores - log_now[:, :, None])
    softmax_low = softmax.astype(jnp.bfloat16)
    score_grad = (scaling * softmax * (prob_grad - mean_now[:, :, None])).astype(jnp.bfloat16)
    query_term = jnp.einsum(
        "hrc,chd->rhd", score_grad, key_heads, preferred_element_type=jnp.float32
    ).reshape(part_query.shape[0], features)
    key_term = jnp.einsum(
        "hrc,rhd->chd", score_grad, query_heads, preferred_element_type=jnp.float32
    ).reshape(key_block.shape[0], features)
    value_term = jnp.einsum(
        "hrc,rhd->chd", softmax_low, grad_heads, preferred_element_type=jnp.float32
    ).reshape(key_block.shape[0], features)
    return (query_term, key_term, value_term)


def on_device(obj_query, grad_out, pattern_key, pattern_value, pencil_order):
    amount, features = obj_query.shape
    columns = pattern_key.shape[0]
    groups = lax.axis_size("grp")
    position = lax.axis_index("grp")
    group_rows = groups * amount
    all_query, all_grad = (
        lax.all_gather(obj_query, "grp", axis=0, tiled=True),
        lax.all_gather(grad_out, "grp", axis=0, tiled=True),
    )
    partial_value = stats_of_rows(all_query, all_grad, pattern_key, pattern_value)
    highest, totals, weighted = joined(partial_value, "grp", join_stats)
    log_totals = highest + jnp.log(totals)
    mean_grads = weighted / totals
    blocking = math.gcd(group_rows, 128)
    sweeps = group_rows // blocking

    def sweep(carried, segment):
        keys_acc, values_acc = carried
        query_term, key_term, value_term = block_grads(
            segment[0], segment[1], segment[2], segment[3], pattern_key, pattern_value
        )
        return ((keys_acc + key_term, values_acc + value_term), query_term)

    log_blocks = jnp.moveaxis(log_totals.reshape(H, sweeps, blocking), 1, 0)
    mean_blocks = jnp.moveaxis(mean_grads.reshape(H, sweeps, blocking), 1, 0)
    zeros_acc = jnp.zeros((columns, features), jnp.float32)
    segments = (
        all_query.reshape(sweeps, blocking, features),
        all_grad.reshape(sweeps, blocking, features),
        log_blocks,
        mean_blocks,
    )
    (keys_acc, values_acc), pieces = lax.scan(sweep, (zeros_acc, zeros_acc), segments)
    query_total = lax.psum_scatter(
        pieces.reshape(group_rows, features), "grp", scatter_dimension=0, tiled=True
    )
    device_rows = columns // lax.axis_size("blk")
    spots = jnp.arange(columns, dtype=jnp.int32)
    target = (spots // device_rows * groups + position) * device_rows + spots % device_rows
    source = (
        jnp.take(pencil_order, target // PENCIL) * PENCIL + target % PENCIL - position * columns
    )
    combined = lax.psum_scatter(
        jnp.concatenate(
            [jnp.take(keys_acc, source, axis=0), jnp.take(values_acc, source, axis=0)], axis=1
        ),
        "blk",
        scatter_dimension=0,
        tiled=True,
    )
    key_grad = combined[:, :features].astype(jnp.bfloat16)
    value_grad = combined[:, features:].astype(jnp.bfloat16)
    return (query_total.astype(jnp.bfloat16), key_grad, value_grad)


MESH = pl.DeviceIdType.MESH
F32 = jnp.float32
BF16 = jnp.bfloat16


def mm(a, b, ca, cb):
    return lax.dot_general(a, b, (((ca,), (cb,)), ((), ())), preferred_element_type=F32)


def turn(x):
    return x.T


def fused(
    n_blk,
    n_grp,
    hd,
    q_ref,
    g_ref,
    k_ref,
    v_ref,
    order_ref,
    out_ref,
    kv_in,
    kvt_own,
    kvt,
    qz,
    qgt_own,
    qgt,
    s_buf,
    d_buf,
    inv_buf,
    probs,
    own_v,
    qst,
    full_q,
    pair_st,
    pair_rv,
    own_st,
    full_kv,
    onehot,
    zst,
    l_s,
    kv_ss,
    kv_rs,
    fw_ss,
    fw_rs,
    z_ss,
    z_rs,
    q_ss,
    q_rs,
    b_ss,
    b_rs,
    p_ss,
    p_rs,
    d_ss,
    d_rs,
    o_ss,
    o_rs,
):
    b = lax.axis_index("blk")
    g = lax.axis_index("grp")
    chips = n_grp // 2
    p = g // 2
    c = g % 2
    partner = 2 * p + 1 - c
    rows = q_ref.shape[0]
    cols = k_ref.shape[0]
    gw = chips * hd
    scaling = 1.0 / math.sqrt(hd)
    expc = scaling * math.log2(math.e)

    def lanes(index, width):
        return pl.ds(pl.multiple_of(index * width, width), width)

    def describe(src, dst, ss, rs, bb, gg):
        return pltpu.make_async_remote_copy(
            src_ref=src,
            dst_ref=dst,
            send_sem=ss,
            recv_sem=rs,
            device_id=(bb, gg),
            device_id_type=MESH,
        )

    started = []

    def remote(*args):
        copy = describe(*args)
        copy.start()
        started.append(copy)
        return copy

    local = []
    for t, ref in enumerate((k_ref, v_ref)):
        local.append(pltpu.make_async_copy(ref.at[:, lanes(b, gw)], kv_in.at[t], l_s.at[t]))
    for t, ref in enumerate((q_ref, g_ref)):
        local.append(
            pltpu.make_async_copy(
                ref.at[:, lanes(b, gw)], qz.at[t, lanes(b, rows), :], l_s.at[2 + t]
            )
        )
    for copy in local:
        copy.start()

    barrier = pltpu.get_barrier_semaphore()
    for d in range(1, n_blk):
        pl.semaphore_signal(barrier, inc=1, device_id=((b + d) % n_blk, g), device_id_type=MESH)
    for e in range(1, chips):
        pl.semaphore_signal(
            barrier, inc=1, device_id=(b, 2 * ((p + e) % chips) + c), device_id_type=MESH
        )
    pl.semaphore_signal(barrier, inc=1, device_id=(b, partner), device_id_type=MESH)

    pl.semaphore_wait(barrier, n_blk + chips - 1)

    z_copies = {}
    kv_copies = {}
    forwards = {}
    for t, ref in enumerate((q_ref, g_ref)):
        for d in range(1, n_blk):
            bb = (b + d) % n_blk
            z_copies[t, d] = remote(
                ref.at[:, lanes(bb, gw)],
                qz.at[t, lanes(b, rows), :],
                z_ss.at[d - 1, t],
                z_rs.at[d - 1, t],
                bb,
                g,
            )
    for t in range(2):
        local[t].wait()
        part = turn(kv_in[t])
        for hl in range(chips):
            kvt_own[hl, t] = part[hd * hl : hd * hl + hd]
        for e in range(1, chips):
            pp = (p + e) % chips
            kv_copies[t, e] = remote(
                kvt_own.at[pp, t],
                kvt.at[g, t],
                kv_ss.at[e - 1, t],
                kv_rs.at[e - 1, t],
                b,
                2 * pp + c,
            )
        forwards[t, 0] = remote(
            kvt_own.at[p, t], kvt.at[g, t], fw_ss.at[0, t], fw_rs.at[0, t], b, partner
        )
    kvt[g] = kvt_own[p]

    row = lax.broadcasted_iota(jnp.int32, (PENCIL, cols), 0)
    col = lax.broadcasted_iota(jnp.int32, (PENCIL, cols), 1)
    per = rows // PENCIL
    for bb in range(n_blk):
        for k in range(per):
            first = order_ref[(bb * n_grp + g) * per + k] * PENCIL - g * cols
            onehot[pl.ds(bb * rows + k * PENCIL, PENCIL), :] = jnp.where(
                col - row == first, 1.0, 0.0
            ).astype(BF16)

    def forward(t):
        for e in range(1, chips):
            src = 2 * ((p - e + chips) % chips) + c
            kv_copies[t, e].wait_recv()
            forwards[t, e] = remote(
                kvt.at[src, t], kvt.at[src, t], fw_ss.at[e, t], fw_rs.at[e, t], b, partner
            )

    def exchange(t):
        local[2 + t].wait()
        for d in range(1, n_blk):
            z_copies[t, d].wait_recv()
        part = turn(qz[t])
        for hl in range(chips):
            qgt_own[hl, t] = part[hd * hl : hd * hl + hd]
        for e in range(1, chips):
            pp = (p + e) % chips
            remote(
                qgt_own.at[pp, t],
                qgt.at[p, t],
                q_ss.at[e - 1, t],
                q_rs.at[e - 1, t],
                b,
                2 * pp + c,
            )
        qgt[p, t] = qgt_own[p, t]

    def arrived(t, e, src):
        describe(
            qgt_own.at[0, t],
            qgt.at[src, t],
            q_ss.at[e - 1, t],
            q_rs.at[e - 1, t],
            b,
            2 * src + c,
        ).wait_recv()

    def from_chip(e):
        return (p - e + chips) % chips

    def back(e, src):
        return describe(
            qst.at[e], full_q.at[p], b_ss.at[e - 1], b_rs.at[e - 1], b, 2 * src + c
        )

    def weights(e, carry):
        src = from_chip(e)

        @pl.when(e > 0)
        def _():
            arrived(0, e, src)

        qb = turn(qgt[src, 0])
        top = jnp.full((cols, cols), -jnp.inf, F32)
        for n in range(n_grp):
            s = mm(qb, kvt[n, 0], 1, 0)
            s_buf[e, n] = s
            top = jnp.maximum(top, s)
        top = jnp.max(top, axis=1, keepdims=True)
        tot = jnp.zeros((cols, cols), F32)
        for n in range(n_grp):
            x = jnp.exp2((s_buf[e, n] - top) * expc)
            s_buf[e, n] = x
            tot = tot + x
        inv_buf[e] = 1.0 / jnp.sum(tot, axis=1, keepdims=True)
        return carry

    def value_sums(n):
        total = jnp.zeros((hd, cols), F32)
        for e in range(chips):
            low = (s_buf[e, n] * inv_buf[e]).astype(BF16)
            total = total + mm(qgt[from_chip(e), 1], low, 1, 0)
        return total

    def key_sums(n):
        total = jnp.zeros((hd, cols), F32)
        for e in range(chips):
            total = total + mm(qgt[from_chip(e), 0], probs[e, n], 1, 0)
        return total

    def grads(e, carry):
        src = from_chip(e)
        gb = turn(qgt[src, 1])
        wtd = jnp.zeros((cols, cols), F32)
        for n in range(n_grp):
            dp = mm(gb, kvt[n, 1], 1, 0)
            d_buf[n] = dp
            wtd = wtd + s_buf[e, n] * dp
        inv = inv_buf[e]
        mean = jnp.sum(wtd, axis=1, keepdims=True) * inv
        acc = jnp.zeros((cols, hd), F32)
        for n in range(n_grp):
            soft = s_buf[e, n] * inv
            sg = (scaling * soft * (d_buf[n] - mean)).astype(BF16)
            probs[e, n] = sg
            acc = acc + mm(sg, kvt[n, 0], 1, 1)
        qst[e] = turn(acc).astype(BF16)

        @pl.when(e > 0)
        def _():
            back(e, src).start()

        return carry

    order = [*range(1, chips), 0]
    pair = {}

    def swap(t, e, total):
        pair_st[e, t] = total.astype(BF16)
        pair[e, t] = remote(
            pair_st.at[e, t], pair_rv.at[e, t], p_ss.at[e, t], p_rs.at[e, t], b, partner
        )

    forward(0)
    exchange(0)
    for e in range(chips):
        forwards[0, e].wait_recv()
    lax.fori_loop(0, 2, weights, 0)
    forward(1)
    exchange(1)
    lax.fori_loop(2, chips, weights, 0)
    for e in range(1, chips):
        arrived(1, e, from_chip(e))
    for e in order:
        swap(1, e, value_sums(2 * ((p + e) % chips) + 1 - c))
    for e in order:
        own_v[e] = value_sums(2 * ((p + e) % chips) + c)
    for e in range(chips):
        forwards[1, e].wait_recv()

    out_copies = []

    def deliver(t, value):
        zst[t] = value
        for d in range(1, n_blk):
            bb = (b + d) % n_blk
            out_copies.append(
                remote(
                    zst.at[t, lanes(bb, rows), :],
                    out_ref.at[t, :, lanes(b, gw)],
                    o_ss.at[d - 1, t],
                    o_rs.at[d - 1, t],
                    bb,
                    g,
                )
            )
        out_ref[t, :, lanes(b, gw)] = zst[t, lanes(b, rows), :]

    home = {}

    def finish(t):
        for e in order:
            pp = (p + e) % chips
            mine = own_v[e] if t else key_sums(2 * pp + c)
            pair[e, t].wait_recv()
            done = (mine + pair_rv[e, t].astype(F32)).astype(BF16)
            if e:
                own_st[e - 1, t] = done
                home[e, t] = remote(
                    own_st.at[e - 1, t],
                    full_kv.at[p, t],
                    d_ss.at[e - 1, t],
                    d_rs.at[e - 1, t],
                    b,
                    2 * pp + c,
                )
            else:
                full_kv[p, t] = done

    def permuted(t):
        for e in range(1, chips):
            home[e, t].wait_recv()
        both = full_kv[:, t].reshape(gw, cols)
        deliver(1 + t, mm(onehot[...], both, 1, 1).astype(BF16))

    finish(1)
    lax.fori_loop(0, 2, grads, 0)
    permuted(1)
    lax.fori_loop(2, chips, grads, 0)
    full_q[p] = qst[0]
    for e in order:
        swap(0, e, key_sums(2 * ((p + e) % chips) + 1 - c))
    finish(0)
    for e in range(1, chips):
        back(e, from_chip(e)).wait_recv()
    deliver(0, turn(full_q[...].reshape(gw, cols)))
    permuted(0)

    for copy in out_copies:
        copy.wait_recv()
    for copy in started:
        copy.wait_send()
    for e in range(1, chips):
        back(e, from_chip(e)).wait_send()


def fused_on_device(n_blk, n_grp, obj_query, grad_out, pattern_key, pattern_value, pencil_order):
    rows, features = obj_query.shape
    cols = pattern_key.shape[0]
    hd = features // H
    chips = n_grp // 2
    gw = chips * hd
    dma = pltpu.SemaphoreType.DMA
    vmem = pl.BlockSpec(memory_space=pltpu.VMEM)
    anywhere = pl.BlockSpec(memory_space=pltpu.HBM)
    joined_out = (
        pl.pallas_call(
            functools.partial(fused, n_blk, n_grp, hd),
            out_shape=jax.ShapeDtypeStruct((3, rows, features), BF16),
            in_specs=[anywhere] * 4 + [pl.BlockSpec(memory_space=pltpu.SMEM)],
            out_specs=vmem,
            scratch_shapes=[
                pltpu.VMEM((2, cols, gw), BF16),
                pltpu.VMEM((chips, 2, hd, cols), BF16),
                pltpu.VMEM((n_grp, 2, hd, cols), BF16),
                pltpu.VMEM((2, cols, gw), BF16),
                pltpu.VMEM((chips, 2, hd, cols), BF16),
                pltpu.VMEM((chips, 2, hd, cols), BF16),
                pltpu.VMEM((chips, n_grp, cols, cols), F32),
                pltpu.VMEM((n_grp, cols, cols), F32),
                pltpu.VMEM((chips, cols, 1), F32),
                pltpu.VMEM((chips, n_grp, cols, cols), BF16),
                pltpu.VMEM((chips, hd, cols), F32),
                pltpu.VMEM((chips, hd, cols), BF16),
                pltpu.VMEM((chips, hd, cols), BF16),
                pltpu.VMEM((chips, 2, hd, cols), BF16),
                pltpu.VMEM((chips, 2, hd, cols), BF16),
                pltpu.VMEM((chips - 1, 2, hd, cols), BF16),
                pltpu.VMEM((chips, 2, hd, cols), BF16),
                pltpu.VMEM((cols, cols), BF16),
                pltpu.VMEM((3, cols, gw), BF16),
                dma((4,)),
                dma((chips - 1, 2)),
                dma((chips - 1, 2)),
                dma((chips, 2)),
                dma((chips, 2)),
                dma((n_blk - 1, 2)),
                dma((n_blk - 1, 2)),
                dma((chips - 1, 2)),
                dma((chips - 1, 2)),
                dma((chips - 1,)),
                dma((chips - 1,)),
                dma((chips, 2)),
                dma((chips, 2)),
                dma((chips - 1, 2)),
                dma((chips - 1, 2)),
                dma((n_blk - 1, 3)),
                dma((n_blk - 1, 3)),
            ],
            compiler_params=pltpu.CompilerParams(
                collective_id=0, has_side_effects=True, vmem_limit_bytes=56 * 1024 * 1024
            ),
        )(obj_query, grad_out, pattern_key, pattern_value, pencil_order)
    )
    return joined_out[0], joined_out[1], joined_out[2]


def solution(mesh):
    in_specs = (
        P(("blk", "grp"), None),
        P(("blk", "grp"), None),
        P("grp", None),
        P("grp", None),
        P(),
    )
    out_specs = (P(("blk", "grp"), None), P(("blk", "grp"), None), P(("blk", "grp"), None))
    n_blk, n_grp = mesh.shape["blk"], mesh.shape["grp"]

    def body(obj_query, grad_out, pattern_key, pattern_value, pencil_order):
        features = obj_query.shape[1]
        fits = (
            n_blk * n_grp // 2 == H
            and (features // n_blk) % 128 == 0
            and pattern_key.shape[0] == 256
            and n_blk * obj_query.shape[0] == 256
        )
        step = functools.partial(fused_on_device, n_blk, n_grp) if fits else on_device
        return step(obj_query, grad_out, pattern_key, pattern_value, pencil_order)

    return jax.shard_map(body, mesh=mesh, in_specs=in_specs, out_specs=out_specs, check_vma=False)
```
